256 devices in a mesh: head: 8 (over z_hi, core), frame: 32 (over z_lo, x, y).
Axes of the slice: x: 4, y: 4, z: 8 (z_hi: 4, z_lo: 2; z = z_hi * 2 + z_lo), core: 2. Of those that a mesh axis runs over, the one named last changes fastest.
Arguments:
- query: bfloat16 [32, 1024, 2048], P('frame', 'head'), may hold values from -5 to 5
- key: bfloat16 [32, 1024, 2048], P('frame', 'head'), may hold values from -5 to 5
- value: bfloat16 [32, 1024, 2048], P('frame', 'head'), may hold values from -6 to 6
- grad_out: bfloat16 [32, 1024, 2048], P('frame', 'head'), may hold values from -6 to 6
- attn_out: bfloat16 [32, 1024, 2048], P('frame', 'head'), may hold values from -6 to 6
- window: int32 [16, 3], replicated, may hold values from 0 to 2, as said below
Outputs:
- grad_query: bfloat16 [32, 1024, 2048], P('frame', 'head')
- grad_key: bfloat16 [32, 1024, 2048], P('frame', 'head')
- grad_value: bfloat16 [32, 1024, 2048], P('frame', 'head')
The draws below stay inside these ranges and needn't reach their ends.
Inputs may be any that keep to these rules, and one draw needn't show every extreme that they name: `window`: column 0 is at most 1, column 1 at most 1, column 2 at most 2; in each column some head takes the largest value and some head takes 0.
All inputs are finite; a program needn't handle non-finite values.
Results may differ from the reference program's by a relative error of at most 0.0053.
Values may be sent and summed in bfloat16 or wider, within the bound.
A program may use at most 128 MiB of HBM per device.

```python
import jax
import jax.numpy as jnp
from jax import lax

HEADS = 16
HD = 128
COLS = 64
TILE = 8
RF = 1
RH = 1
RW = 2
TOKF = 1024
FRAMES = 32


def aligned_parts(key):
    signs = jnp.where(jax.random.bernoulli(key, 0.5, (FRAMES, TOKF, HEADS * HD)), 1.0, -1.0).astype(jnp.float32)
    return signs


def draw_query(key, part):
    signs = aligned_parts(key)
    key = jax.random.fold_in(key, 3)
    base = jnp.clip(jax.random.normal(key, signs.shape, jnp.float32), -5.0, 5.0)
    return base.astype(jnp.bfloat16)


def draw_key(key, part):
    signs = aligned_parts(key)
    key = jax.random.fold_in(key, 5)
    base = jnp.clip(jax.random.normal(key, signs.shape, jnp.float32), -5.0, 5.0)
    return base.astype(jnp.bfloat16)


def draw_window(key, part):
    key = jax.random.fold_in(key, 11)
    columns = []
    for column, largest in enumerate((RF, RH, RW)):
        subkey = jax.random.fold_in(key, column)
        picks = jax.random.randint(subkey, (HEADS,), 0, largest + 1)
        order = jax.random.permutation(jax.random.fold_in(subkey, 7), HEADS)
        picks = picks.at[order[0]].set(largest).at[order[1]].set(0)
        columns.append(picks)
    return jnp.stack(columns, axis=1).astype(jnp.int32)


def block_scale(key, extent, cuts, least, high):
    def one(position, shards_of):
        heights = jax.random.uniform(jax.random.fold_in(jax.random.fold_in(key, 6), position), (shards_of,), jnp.float32, least / len(cuts), high / len(cuts))
        return jnp.repeat(jnp.exp(heights), extent[position] // shards_of).reshape((-1,) + (1,) * (len(extent) - position - 1))

    factor_of = one(*cuts[0])
    for cut in cuts[1:]:
        factor_of = factor_of * one(*cut)
    return factor_of


def noise(key, extent, spread, most, pieces=(), kind=jnp.bfloat16):
    drawn = spread * jax.random.normal(key, extent, jnp.float32)
    if pieces:
        drawn = drawn * block_scale(key, extent, pieces, -0.22, 0.18)
    return jnp.clip(drawn, -most, most).astype(kind)


def setup_inputs(seed: int = 0) -> dict:
    seeds = jax.random.split(jax.random.key(seed), 7)
    return {
        "query": draw_query(jax.random.fold_in(seeds[6], 71), 0),
        "key": draw_key(jax.random.fold_in(seeds[6], 71), 0),
        "value": noise(seeds[2], (FRAMES, TOKF, HEADS * HD), 1.0, 6.0, ((0, 32), (1, 8))),
        "grad_out": noise(seeds[3], (FRAMES, TOKF, HEADS * HD), 1.0, 6.0, ((0, 32), (1, 8))),
        "attn_out": noise(seeds[4], (FRAMES, TOKF, HEADS * HD), 1.0, 6.0, ((0, 32), (1, 8))),
        "window": draw_window(jax.random.fold_in(seeds[6], 71), 0),
    }


def split_heads(array):
    return array.reshape(FRAMES, TOKF, HEADS, HD).transpose(2, 0, 1, 3)


def join_heads(array):
    return array.transpose(1, 2, 0, 3).reshape(FRAMES, TOKF, HEADS * HD)


def contract(left, right, left_dim, right_dim):
    return lax.dot_general(left, right, (((left_dim,), (right_dim,)), ((), ())), preferred_element_type=jnp.float32)


def add_frame(accum, part, where_at):
    current = lax.dynamic_slice_in_dim(accum, where_at, 1, 0)
    return lax.dynamic_update_slice_in_dim(accum, current + part[None], where_at, 0)


def reference(query, key, value, grad_out, attn_out, window):
    scale = HD ** -0.5
    positions = jnp.arange(TOKF, dtype=jnp.int32)
    tile_row = (positions // COLS) // TILE
    tile_col = (positions % COLS) // TILE
    row_gap = jnp.abs(tile_row[:, None] - tile_row[None, :])
    col_gap = jnp.abs(tile_col[:, None] - tile_col[None, :])
    product = grad_out.astype(jnp.float32).reshape(FRAMES, TOKF, HEADS, HD) * attn_out.astype(jnp.float32).reshape(FRAMES, TOKF, HEADS, HD)
    deltas = jnp.sum(product, axis=3).transpose(2, 0, 1)
    padding = jnp.zeros((RF, TOKF, HD), jnp.bfloat16)
    offsets = list(range(-RF, RF + 1))

    def one_head(items):
        queries, keys, values, grads, delta_head, reach = items
        keys_pad = jnp.concatenate([padding, keys, padding], axis=0)
        values_pad = jnp.concatenate([padding, values, padding], axis=0)
        spatial = (row_gap <= reach[1]) & (col_gap <= reach[2])

        def one_frame(carry, frame):
            key_acc, value_acc = carry
            own_q = lax.dynamic_index_in_dim(queries, frame, 0, keepdims=False)
            own_g = lax.dynamic_index_in_dim(grads, frame, 0, keepdims=False)
            own_delta = lax.dynamic_index_in_dim(delta_head, frame, 0, keepdims=False)
            masked = []
            remote = []
            for offset in offsets:
                where_at = (frame + offset + RF).astype(jnp.int32)
                far_keys = lax.dynamic_index_in_dim(keys_pad, where_at, 0, keepdims=False)
                far_values = lax.dynamic_index_in_dim(values_pad, where_at, 0, keepdims=False)
                valid = (frame + offset >= 0) & (frame + offset < FRAMES) & (abs(offset) <= reach[0])
                raw = contract(own_q, far_keys, 1, 1) * scale
                masked.append(jnp.where(spatial & valid, raw, -jnp.inf))
                remote.append((where_at, far_keys, far_values))
            joined = jnp.concatenate(masked, axis=1)
            top = jnp.max(joined, axis=1)
            log_total = top + jnp.log(jnp.sum(jnp.exp(joined - top[:, None]), axis=1))
            grad_q = jnp.zeros((TOKF, HD), jnp.float32)
            for index, offset in enumerate(offsets):
                where_at, far_keys, far_values = remote[index]
                prob = jnp.exp(masked[index] - log_total[:, None])
                prob_half = prob.astype(jnp.bfloat16)
                value_part = contract(prob_half, own_g, 0, 0)
                prob_grad = contract(own_g, far_values, 1, 1)
                score_grad = (prob * (prob_grad - own_delta[:, None])).astype(jnp.bfloat16)
                grad_q = grad_q + jnp.dot(score_grad, far_keys, preferred_element_type=jnp.float32)
                key_part = contract(score_grad, own_q, 0, 0) * scale
                if offset != 0:
                    key_part = lax.optimization_barrier(key_part.astype(jnp.bfloat16)).astype(jnp.float32)
                    value_part = lax.optimization_barrier(value_part.astype(jnp.bfloat16)).astype(jnp.float32)
                key_acc = add_frame(key_acc, key_part, where_at)
                value_acc = add_frame(value_acc, value_part, where_at)
            return (key_acc, value_acc), (grad_q * scale).astype(jnp.bfloat16)

        start = jnp.zeros((FRAMES + 2 * RF, TOKF, HD), jnp.float32)
        (key_acc, value_acc), grad_q = lax.scan(one_frame, (start, start), jnp.arange(FRAMES, dtype=jnp.int32))
        grad_k = key_acc[RF:RF + FRAMES].astype(jnp.bfloat16)
        grad_v = value_acc[RF:RF + FRAMES].astype(jnp.bfloat16)
        return grad_q, grad_k, grad_v

    grad_q, grad_k, grad_v = lax.map(one_head, (split_heads(query), split_heads(key), split_heads(value), split_heads(grad_out), deltas, window))
    return join_heads(grad_q), join_heads(grad_k), join_heads(grad_v)
```

```python
import functools

import jax
import jax.numpy as jnp
from jax import lax
from jax.experimental import pallas as pl
from jax.experimental.pallas import tpu as pltpu
from jax.sharding import PartitionSpec as P

COLS = 64
TILE = 8
MESH = pl.DeviceIdType.MESH
FAR = -1e30
K, V, Q, G = range(4)


def dot(left, right):
    return jnp.dot(left, right, preferred_element_type=jnp.float32)


def dot_nt(left, right):
    return lax.dot_general(left, right, (((1,), (1,)), ((), ())), preferred_element_type=jnp.float32)


def kernel(
    heads,
    groups,
    frames,
    window_ref,
    k_ref,
    v_ref,
    q_ref,
    g_ref,
    o_ref,
    dq_ref,
    dk_ref,
    dv_ref,
    g_own,
    o_own,
    delta_out,
    delta_in,
    kv,
    qg,
    k_turned,
    bias,
    scores,
    dq_turned,
    acc,
    parts,
    back,
    zout,
    own_sems,
    delta_sems,
    zin_send,
    zin_recv,
    halo_send,
    halo_recv,
    back_send,
    back_recv,
    zout_send,
    zout_recv,
):
    per_group = heads // groups
    width = kv.shape[-1]
    scale = width**-0.5
    me = lax.axis_index("head")
    here = lax.axis_index("frame")
    across = lax.rem(here + frames // 2, frames)
    up = lax.rem(here + 1, frames)
    down = lax.rem(here + frames - 1, frames)
    pairs = kv.shape[5]
    size = groups * kv.shape[4] * kv.shape[6]

    own = [
        pltpu.make_async_copy(g_ref, g_own, own_sems.at[0]),
        pltpu.make_async_copy(o_ref, o_own, own_sems.at[1]),
    ]
    for copy in own:
        copy.start()

    barrier = pltpu.get_barrier_semaphore()
    for step in range(groups):
        pl.semaphore_signal(
            barrier, 1, device_id=(lax.rem(me + step, groups), across), device_id_type=MESH
        )
    for other in (up, down):
        pl.semaphore_signal(barrier, 1, device_id=(me, other), device_id_type=MESH)
    pl.semaphore_wait(barrier, groups + 2)

    def landing(array, head):
        return kv.at[0, array, head] if array < 2 else qg.at[array - 2, head]

    for head in range(per_group):
        for array, ref in ((K, k_ref), (V, v_ref), (Q, q_ref), (G, g_ref)):
            for step in range(groups):
                to = lax.rem(me + step, groups)
                column = pl.multiple_of((to * per_group + head) * width, width)
                pltpu.make_async_remote_copy(
                    src_ref=ref.at[:, :, :, pl.ds(column, width)],
                    dst_ref=landing(array, head).at[me],
                    send_sem=zin_send.at[array, head],
                    recv_sem=zin_recv.at[array, head],
                    device_id=(to, across),
                    device_id_type=MESH,
                ).start()

    def arrived(array, head):
        ref = landing(array, head)
        pltpu.make_async_copy(ref, ref, zin_recv.at[array, head]).wait()

    for copy in own:
        copy.wait()
    lane = lax.broadcasted_iota(jnp.int32, (1, 128), 1)
    place = lax.rem(me, 4) * 32
    for h in range(heads):
        cols = slice(h * width, (h + 1) * width)
        product = g_own[:, :, :, cols].astype(jnp.float32) * o_own[:, :, :, cols].astype(jnp.float32)
        turned = product.reshape(128, width).T
        row = jnp.sum(turned, axis=0, keepdims=True)
        for m in range(pairs):
            first = pltpu.roll(row, lax.rem(place + 128 - m * 16, 128), 1)
            second = pltpu.roll(row, lax.rem(place + 16 + 64 - m * 16, 128), 1)
            mine = lane - place
            placed = jnp.where(
                (mine >= 0) & (mine < 16),
                first,
                jnp.where((mine >= 16) & (mine < 32), second, 0.0),
            )
            at = (h % per_group) * pairs + m
            delta_out[h // per_group, at : at + 1, :] = placed
    for step in range(groups):
        to = lax.rem(me + step, groups)
        pltpu.make_async_remote_copy(
            src_ref=delta_out.at[to],
            dst_ref=delta_in.at[me],
            send_sem=delta_sems.at[0],
            recv_sem=delta_sems.at[1],
            device_id=(to, across),
            device_id_type=MESH,
        ).start()

    k_at = lax.broadcasted_iota(jnp.int32, (size, size), 0)
    q_at = lax.broadcasted_iota(jnp.int32, (size, size), 1)
    row_gap = jnp.abs(k_at // (size // 2) - q_at // (size // 2))
    frame = across
    for head in range(per_group):
        reach_f = window_ref[me * per_group + head, 0]
        reach_h = window_ref[me * per_group + head, 1]
        reach_w = window_ref[me * per_group + head, 2]
        low = jnp.where((reach_f >= 1) & (frame >= 1), 0.0, FAR)
        high = jnp.where((reach_f >= 1) & (frame < frames - 1), 0.0, FAR)
        for gap in (-1, 0, 1):
            col_gap = jnp.abs(2 * gap + (k_at % 16) // 8 - (q_at % 16) // 8)
            near = jnp.where((row_gap <= reach_h) & (col_gap <= reach_w), 0.0, FAR)
            bias[head, 0, gap + 1] = near
            bias[head, 1, gap + 1] = near + low
            bias[head, 2, gap + 1] = near + high

    def halo(array, head, side):
        return pltpu.make_async_remote_copy(
            src_ref=kv.at[0, array, head],
            dst_ref=kv.at[1 + side, array, head],
            send_sem=halo_send.at[side, array, head],
            recv_sem=halo_recv.at[side, array, head],
            device_id=(me, (up, down)[side]),
            device_id_type=MESH,
        )

    def send_halo(head):
        for array in (K, V):
            arrived(array, head)
            for side in range(2):
                halo(array, head, side).start()

    def part_back(head, n, side):
        return pltpu.make_async_remote_copy(
            src_ref=parts.at[side, head, n],
            dst_ref=back.at[side, head, n],
            send_sem=back_send.at[side, head, n],
            recv_sem=back_recv.at[side, head, n],
            device_id=(me, (down, up)[side]),
            device_id_type=MESH,
        )

    outs = (dq_ref, dk_ref, dv_ref)

    def send_out(array, head, first, count):
        for step in range(groups):
            to = lax.rem(me + step, groups)
            column = pl.multiple_of((me * per_group + head) * width, width)
            pltpu.make_async_remote_copy(
                src_ref=zout.at[array, head, to, :, first : first + count],
                dst_ref=outs[array].at[:, first : first + count, :, pl.ds(column, width)],
                send_sem=zout_send.at[array],
                recv_sem=zout_recv.at[array],
                device_id=(to, across),
                device_id_type=MESH,
            ).start()

    def block(ref, n):
        return ref[:, :, n].reshape(size, width)

    def turn(head, o):
        for n in range(pairs):
            k_turned[o, n] = block(kv.at[o, K, head], n).T

    def compute(head, pieces):
        for m in range(pairs):
            near = [n for n in (m - 1, m, m + 1) if 0 <= n < pairs]
            queries = block(qg.at[0, head], m)
            grads = block(qg.at[1, head], m)
            at = head * pairs + m
            halves = [
                sum(delta_in[s, at : at + 1, :] for s in range(half * 4, half * 4 + 4)) for half in range(2)
            ]
            delta = jnp.concatenate(halves, axis=1)

            def score(o, top):
                for n in near:
                    raw = dot_nt(block(kv.at[o, K, head], n), queries)
                    masked = raw * scale + bias[head, o, n - m + 1]
                    scores[o, n - m + 1] = masked
                    top = jnp.maximum(top, jnp.max(masked.reshape(size // 8, 8, size), axis=0))
                return top

            top = lax.fori_loop(0, 3, score, jnp.full((8, size), FAR, jnp.float32))
            top = jnp.max(top, axis=0, keepdims=True)

            def weight(o, total):
                for n in near:
                    e = jnp.exp(scores[o, n - m + 1] - top)
                    scores[o, n - m + 1] = e
                    total = total + jnp.sum(e.reshape(size // 8, 8, size), axis=0)
                return total

            total = lax.fori_loop(0, 3, weight, jnp.zeros((8, size), jnp.float32))
            inverse = 1.0 / jnp.sum(total, axis=0, keepdims=True)
            dq_turned[...] = jnp.zeros_like(dq_turned)

            def backward(o, nothing):
                for n in near:
                    prob = scores[o, n - m + 1] * inverse
                    prob_grad = dot_nt(block(kv.at[o, V, head], n), grads)
                    score_grad = (prob * (prob_grad - delta)).astype(jnp.bfloat16)
                    key_part = dot(score_grad, queries)
                    value_part = dot(prob.astype(jnp.bfloat16), grads)
                    if m == max(n - 1, 0):
                        acc[head, o, 0, n] = key_part
                        acc[head, o, 1, n] = value_part
                    else:
                        acc[head, o, 0, n] += key_part
                        acc[head, o, 1, n] += value_part
                    dq_turned[...] += dot(k_turned[o, n], score_grad)
                return nothing

            lax.fori_loop(0, 3, backward, 0)
            zout[0, head, :, :, m] = (
                (dq_turned[...] * scale).T.astype(jnp.bfloat16).reshape(zout.shape[2], zout.shape[3], 16, width)
            )
            done = [m - 1] if m < pairs - 1 else [m - 1, m]
            for n in done:
                if n < 0:
                    continue
                for side in range(2):
                    parts[side, head, n, 0] = (acc[head, 1 + side, 0, n] * scale).astype(jnp.bfloat16)
                    parts[side, head, n, 1] = acc[head, 1 + side, 1, n].astype(jnp.bfloat16)
                    part_back(head, n, side).start()
            step = pairs // pieces
            if (m + 1) % step == 0:
                send_out(0, head, m + 1 - step, step)

    def finish(head, pieces):
        step = pairs // pieces
        for n in range(pairs):
            for side in range(2):
                part_back(head, n, side).wait_recv()
            for array in range(2):
                mine = acc[head, 0, array, n]
                if array == 0:
                    mine = mine * scale
                whole = mine + back[0, head, n, array].astype(jnp.float32) + back[1, head, n, array].astype(jnp.float32)
                zout[1 + array, head, :, :, n] = whole.astype(jnp.bfloat16).reshape(
                    zout.shape[2], zout.shape[3], 16, width
                )
            if (n + 1) % step == 0:
                for array in range(2):
                    send_out(1 + array, head, n + 1 - step, step)

    pltpu.make_async_copy(delta_in, delta_in, delta_sems.at[1]).wait()
    for head in range(per_group):
        send_halo(head)
        turn(head, 0)
        if head > 0:
            finish(head - 1, 1)
        arrived(Q, head)
        arrived(G, head)
        for side in range(2):
            for array in (K, V):
                halo(array, head, side).wait_recv()
            turn(head, 1 + side)
        compute(head, 1 if head < per_group - 1 else 2)
    finish(per_group - 1, 2)

    for array in range(3):
        pltpu.make_async_copy(outs[array], outs[array], zout_recv.at[array]).wait()
    for array in range(3):
        pltpu.make_async_copy(zout.at[array], zout.at[array], zout_send.at[array]).wait()
    pltpu.make_async_copy(delta_out, delta_out, delta_sems.at[0]).wait()
    for head in range(per_group):
        for array in (K, V, Q, G):
            ref = landing(array, head)
            pltpu.make_async_copy(ref, ref, zin_send.at[array, head]).wait()
        for side in range(2):
            for array in (K, V):
                halo(array, head, side).wait_send()
            for n in range(pairs):
                part_back(head, n, side).wait_send()


def on_device(query, key, value, grad_out, attn_out, window):
    heads = window.shape[0]
    groups = lax.axis_size("head")
    frames = lax.axis_size("frame")
    tokens = query.shape[1]
    width = query.shape[2] // heads
    per_group = heads // groups
    rows = tokens // COLS
    pairs = COLS // (2 * TILE)
    split = (rows, pairs, 2 * TILE, query.shape[2])
    size = groups * rows * 2 * TILE
    dma = pltpu.SemaphoreType.DMA
    half = jnp.bfloat16
    full = jnp.float32
    any_space = pl.BlockSpec(memory_space=pl.ANY)
    grid = (groups, rows, pairs, 2 * TILE, width)
    outs = pl.pallas_call(
        functools.partial(kernel, heads, groups, frames),
        out_shape=[jax.ShapeDtypeStruct(split, half)] * 3,
        in_specs=[pl.BlockSpec(memory_space=pltpu.SMEM)] + [any_space] * 5,
        out_specs=[any_space] * 3,
        scratch_shapes=[
            pltpu.VMEM(split, half),
            pltpu.VMEM(split, half),
            pltpu.VMEM((groups, per_group * pairs, 128), full),
            pltpu.VMEM((groups, per_group * pairs, 128), full),
            pltpu.VMEM((3, 2, per_group) + grid, half),
            pltpu.VMEM((2, per_group) + grid, half),
            pltpu.VMEM((3, pairs, width, size), half),
            pltpu.VMEM((per_group, 3, 3, size, size), full),
            pltpu.VMEM((3, 3, size, size), full),
            pltpu.VMEM((width, size), full),
            pltpu.VMEM((per_group, 3, 2, pairs, size, width), full),
            pltpu.VMEM((2, per_group, pairs, 2, size, width), half),
            pltpu.VMEM((2, per_group, pairs, 2, size, width), half),
            pltpu.VMEM((3, per_group) + grid, half),
            dma((2,)),
            dma((2,)),
            dma((4, per_group)),
            dma((4, per_group)),
            dma((2, 2, per_group)),
            dma((2, 2, per_group)),
            dma((2, per_group, pairs)),
            dma((2, per_group, pairs)),
            dma((3,)),
            dma((3,)),
        ],
        compiler_params=pltpu.CompilerParams(
            collective_id=0, has_side_effects=True, vmem_limit_bytes=48 * 2**20
        ),
        name="tile_attention_backward",
    )(window, *(x.reshape(split) for x in (key, value, query, grad_out, attn_out)))
    return tuple(x.reshape(query.shape) for x in outs)


def solution(mesh):
    in_specs = (
        P("frame", "head", None),
        P("frame", "head", None),
        P("frame", "head", None),
        P("frame", "head", None),
        P("frame", "head", None),
        P(),
    )
    out_specs = (P("frame", "head", None), P("frame", "head", None), P("frame", "head", None))
    return jax.shard_map(
        on_device, mesh=mesh, in_specs=in_specs, out_specs=out_specs, check_vma=False
    )
```

```python
import functools

import jax
import jax.numpy as jnp
from jax import lax
from jax.experimental import pallas as pl
from jax.experimental.pallas import tpu as pltpu
from jax.sharding import PartitionSpec as P

COLS = 64
TILE = 8
MESH = pl.DeviceIdType.MESH
FAR = -1e30
K, V, Q, G = range(4)


def dot(left, right):
    return jnp.dot(left, right, preferred_element_type=jnp.float32)


def dot_nt(left, right):
    return lax.dot_general(left, right, (((1,), (1,)), ((), ())), preferred_element_type=jnp.float32)


def kernel(
    heads,
    groups,
    frames,
    window_ref,
    k_ref,
    v_ref,
    q_ref,
    g_ref,
    o_ref,
    dq_ref,
    dk_ref,
    dv_ref,
    g_own,
    o_own,
    delta_out,
    delta_in,
    kv,
    qg,
    k_turned,
    bias,
    scores,
    dq_turned,
    acc,
    parts,
    back,
    zout,
    own_sems,
    delta_sems,
    zin_send,
    zin_recv,
    halo_send,
    halo_recv,
    back_send,
    back_recv,
    zout_send,
    zout_recv,
):
    per_group = heads // groups
    width = kv.shape[-1]
    scale = width**-0.5
    me = lax.axis_index("head")
    here = lax.axis_index("frame")
    spots = frames // 2
    low, spot = here // spots, lax.rem(here, spots)
    high, core = me // 2, lax.rem(me, 2)
    frame = core * spots + spot
    group = high * 2 + low
    same = core == low
    pairs = kv.shape[5]
    size = groups * kv.shape[4] * kv.shape[6]

    def worker(g):
        return (g // 2 * 2 + low, lax.rem(g, 2) * spots + spot)

    def neighbour(f):
        return (high * 2 + f // spots, low * spots + lax.rem(f, spots))

    up = neighbour(lax.rem(frame + 1, frames))
    down = neighbour(lax.rem(frame + frames - 1, frames))

    own = [
        pltpu.make_async_copy(g_ref, g_own, own_sems.at[0]),
        pltpu.make_async_copy(o_ref, o_own, own_sems.at[1]),
    ]
    for copy in own:
        copy.start()

    barrier = pltpu.get_barrier_semaphore()

    @pl.when(jnp.logical_not(same))
    def _():
        pl.semaphore_signal(barrier, 1, device_id=worker(group), device_id_type=MESH)

    for step in range(1, groups):
        pl.semaphore_signal(
            barrier, 1, device_id=worker(lax.rem(group + step, groups)), device_id_type=MESH
        )
    for i in range(groups // 2):
        pl.semaphore_signal(barrier, 1, device_id=(2 * i + 1 - low, frame), device_id_type=MESH)
    for other in (up, down):
        pl.semaphore_signal(barrier, 1, device_id=other, device_id_type=MESH)
    pl.semaphore_wait(barrier, groups - 1 + groups // 2 + 2 + jnp.where(same, 0, 1))

    def landing(array, head):
        return kv.at[0, array, head] if array < 2 else qg.at[array - 2, head]

    def move(step, src, dst, send, recv, to):
        def remote():
            pltpu.make_async_remote_copy(
                src_ref=src, dst_ref=dst, send_sem=send, recv_sem=recv, device_id=to, device_id_type=MESH
            ).start()

        if step > 0:
            remote()
        else:
            pl.when(jnp.logical_not(same))(remote)

            @pl.when(same)
            def _():
                pltpu.make_async_copy(src, dst, recv).start()

    def wait_sent(ref, sem):
        rest = ref.at[1:groups]
        pltpu.make_async_copy(rest, rest, sem).wait()

        @pl.when(jnp.logical_not(same))
        def _():
            pltpu.make_async_copy(ref.at[0], ref.at[0], sem).wait()

    def send_in(array, head):
        ref = (k_ref, v_ref, q_ref, g_ref)[array]
        for step in range(groups):
            to = lax.rem(group + step, groups)
            column = pl.multiple_of((to * per_group + head) * width, width)
            move(
                step,
                ref.at[:, :, :, pl.ds(column, width)],
                landing(array, head).at[me],
                zin_send.at[array, head],
                zin_recv.at[array, head],
                worker(to),
            )

    def arrived(array, head):
        ref = landing(array, head)
        pltpu.make_async_copy(ref, ref, zin_recv.at[array, head]).wait()

    for array in (K, V, Q):
        send_in(array, 0)

    for copy in own:
        copy.wait()
    lane = lax.broadcasted_iota(jnp.int32, (1, 128), 1)
    place = lax.rem(me, 4) * 32
    for h in range(heads):
        cols = slice(h * width, (h + 1) * width)
        product = g_own[:, :, :, cols].astype(jnp.float32) * o_own[:, :, :, cols].astype(jnp.float32)
        turned = product.reshape(128, width).T
        row = jnp.sum(turned, axis=0, keepdims=True)
        for m in range(pairs):
            first = pltpu.roll(row, lax.rem(place + 128 - m * 16, 128), 1)
            second = pltpu.roll(row, lax.rem(place + 16 + 64 - m * 16, 128), 1)
            mine = lane - place
            placed = jnp.where(
                (mine >= 0) & (mine < 16),
                first,
                jnp.where((mine >= 16) & (mine < 32), second, 0.0),
            )
            at = (h % per_group) * pairs + m
            delta_out[h // per_group, at : at + 1, :] = placed
    for step in range(groups):
        to = lax.rem(group + step, groups)
        move(step, delta_out.at[to], delta_in.at[me], delta_sems.at[0], delta_sems.at[1], worker(to))

    k_at = lax.broadcasted_iota(jnp.int32, (size, size), 0)
    q_at = lax.broadcasted_iota(jnp.int32, (size, size), 1)
    row_gap = jnp.abs(k_at // (size // 2) - q_at // (size // 2))
    for head in range(per_group):
        reach_f = window_ref[group * per_group + head, 0]
        reach_h = window_ref[group * per_group + head, 1]
        reach_w = window_ref[group * per_group + head, 2]
        below = jnp.where((reach_f >= 1) & (frame >= 1), 0.0, FAR)
        above = jnp.where((reach_f >= 1) & (frame < frames - 1), 0.0, FAR)
        for gap in (-1, 0, 1):
            col_gap = jnp.abs(2 * gap + (k_at % 16) // 8 - (q_at % 16) // 8)
            near = jnp.where((row_gap <= reach_h) & (col_gap <= reach_w), 0.0, FAR)
            bias[head, 0, gap + 1] = near
            bias[head, 1, gap + 1] = near + below
            bias[head, 2, gap + 1] = near + above

    def halo(array, head, side):
        return pltpu.make_async_remote_copy(
            src_ref=kv.at[0, array, head],
            dst_ref=kv.at[1 + side, array, head],
            send_sem=halo_send.at[side, array, head],
            recv_sem=halo_recv.at[side, array, head],
            device_id=(up, down)[side],
            device_id_type=MESH,
        )

    def send_halo(array, head):
        arrived(array, head)
        for side in range(2):
            halo(array, head, side).start()

    def part_back(head, n, side):
        return pltpu.make_async_remote_copy(
            src_ref=parts.at[side, head, n],
            dst_ref=back.at[side, head, n],
            send_sem=back_send.at[side, head, n],
            recv_sem=back_recv.at[side, head, n],
            device_id=(down, up)[side],
            device_id_type=MESH,
        )

    outs = (dq_ref, dk_ref, dv_ref)

    def send_out(array, head, first, count):
        for step in range(groups):
            to = lax.rem(me + step, groups)
            column = pl.multiple_of((group * per_group + head) * width, width)
            move(
                step,
                zout.at[array, head, to, :, first : first + count],
                outs[array].at[:, first : first + count, :, pl.ds(column, width)],
                zout_send.at[array, head],
                zout_recv.at[array],
                (to, frame),
            )

    def block(ref, n):
        return ref[:, :, n].reshape(size, width)

    def turn(head, o):
        for n in range(pairs):
            k_turned[o, n] = block(kv.at[o, K, head], n).T

    def compute(head, pieces, after):
        for m in range(pairs):
            near = [n for n in (m - 1, m, m + 1) if 0 <= n < pairs]
            queries = block(qg.at[0, head], m)
            grads = block(qg.at[1, head], m)
            at = head * pairs + m
            halves = [
                sum(delta_in[s, at : at + 1, :] for s in range(half * 4, half * 4 + 4)) for half in range(2)
            ]
            delta = jnp.concatenate(halves, axis=1)

            def score(o, top):
                for n in near:
                    raw = dot_nt(block(kv.at[o, K, head], n), queries)
                    masked = raw * scale + bias[head, o, n - m + 1]
                    scores[o, n - m + 1] = masked
                    top = jnp.maximum(top, jnp.max(masked.reshape(size // 8, 8, size), axis=0))
                return top

            top = lax.fori_loop(0, 3, score, jnp.full((8, size), FAR, jnp.float32))
            top = jnp.max(top, axis=0, keepdims=True)

            def weight(o, total):
                for n in near:
                    e = jnp.exp(scores[o, n - m + 1] - top)
                    scores[o, n - m + 1] = e
                    total = total + jnp.sum(e.reshape(size // 8, 8, size), axis=0)
                return total

            total = lax.fori_loop(0, 3, weight, jnp.zeros((8, size), jnp.float32))
            inverse = 1.0 / jnp.sum(total, axis=0, keepdims=True)
            dq_turned[...] = jnp.zeros_like(dq_turned)

            def backward(o, nothing):
                for n in near:
                    prob = scores[o, n - m + 1] * inverse
                    prob_grad = dot_nt(block(kv.at[o, V, head], n), grads)
                    score_grad = (prob * (prob_grad - delta)).astype(jnp.bfloat16)
                    key_part = dot(score_grad, queries)
                    value_part = dot(prob.astype(jnp.bfloat16), grads)
                    if m == max(n - 1, 0):
                        acc[head, o, 0, n] = key_part
                        acc[head, o, 1, n] = value_part
                    else:
                        acc[head, o, 0, n] += key_part
                        acc[head, o, 1, n] += value_part
                    dq_turned[...] += dot(k_turned[o, n], score_grad)
                return nothing

            lax.fori_loop(0, 3, backward, 0)
            zout[0, head, :, :, m] = (
                (dq_turned[...] * scale).T.astype(jnp.bfloat16).reshape(zout.shape[2], zout.shape[3], 16, width)
            )
            done = [m - 1] if m < pairs - 1 else [m - 1, m]
            for n in done:
                if n < 0:
                    continue
                for side in range(2):
                    parts[side, head, n, 0] = (acc[head, 1 + side, 0, n] * scale).astype(jnp.bfloat16)
                    parts[side, head, n, 1] = acc[head, 1 + side, 1, n].astype(jnp.bfloat16)
                    part_back(head, n, side).start()
            step = pairs // pieces
            if (m + 1) % step == 0:
                send_out(0, head, m + 1 - step, step)
            after(m)

    def finish(head, first, count):
        for n in range(first, first + count):
            for side in range(2):
                part_back(head, n, side).wait_recv()
            for array in range(2):
                mine = acc[head, 0, array, n]
                if array == 0:
                    mine = mine * scale
                whole = mine + back[0, head, n, array].astype(jnp.float32) + back[1, head, n, array].astype(jnp.float32)
                zout[1 + array, head, :, :, n] = whole.astype(jnp.bfloat16).reshape(
                    zout.shape[2], zout.shape[3], 16, width
                )
        for array in range(2):
            send_out(1 + array, head, first, count)

    def halo_arrived(array, head):
        for side in range(2):
            halo(array, head, side).wait_recv()

    half = pairs // 2
    send_halo(K, 0)
    send_in(G, 0)
    turn(0, 0)
    send_halo(V, 0)
    send_in(K, 1)
    arrived(Q, 0)
    send_in(V, 1)
    halo_arrived(K, 0)
    turn(0, 1)
    turn(0, 2)
    pltpu.make_async_copy(delta_in, delta_in, delta_sems.at[1]).wait()
    arrived(G, 0)
    send_in(Q, 1)
    halo_arrived(V, 0)

    def during_first(m):
        if m == 1:
            send_halo(K, 1)
            send_in(G, 1)
        elif m == pairs - 1:
            send_halo(V, 1)

    compute(0, 1, during_first)
    turn(1, 0)
    finish(0, 0, half)
    halo_arrived(K, 1)
    turn(1, 1)
    turn(1, 2)
    arrived(Q, 1)
    arrived(G, 1)
    halo_arrived(V, 1)

    def during_second(m):
        if m == 0:
            finish(0, half, half)

    compute(1, 2, during_second)
    finish(1, 0, half)
    finish(1, half, half)

    for array in range(3):
        pltpu.make_async_copy(outs[array], outs[array], zout_recv.at[array]).wait()
    for head in range(per_group):
        for array in range(3):
            wait_sent(zout.at[array, head], zout_send.at[array, head])
        for array in (K, V, Q, G):
            wait_sent(landing(array, head), zin_send.at[array, head])
        for side in range(2):
            for array in (K, V):
                halo(array, head, side).wait_send()
            for n in range(pairs):
                part_back(head, n, side).wait_send()
    wait_sent(delta_out, delta_sems.at[0])


def on_device(query, key, value, grad_out, attn_out, window):
    heads = window.shape[0]
    groups = lax.axis_size("head")
    frames = lax.axis_size("frame")
    tokens = query.shape[1]
    width = query.shape[2] // heads
    per_group = heads // groups
    rows = tokens // COLS
    pairs = COLS // (2 * TILE)
    split = (rows, pairs, 2 * TILE, query.shape[2])
    size = groups * rows * 2 * TILE
    dma = pltpu.SemaphoreType.DMA
    half = jnp.bfloat16
    full = jnp.float32
    in_hbm = pl.BlockSpec(memory_space=pltpu.HBM)
    grid = (groups, rows, pairs, 2 * TILE, width)
    outs = pl.pallas_call(
        functools.partial(kernel, heads, groups, frames),
        out_shape=[jax.ShapeDtypeStruct(split, half)] * 3,
        in_specs=[pl.BlockSpec(memory_space=pltpu.SMEM)] + [in_hbm] * 5,
        out_specs=[in_hbm] * 3,
        scratch_shapes=[
            pltpu.VMEM(split, half),
            pltpu.VMEM(split, half),
            pltpu.VMEM((groups, per_group * pairs, 128), full),
            pltpu.VMEM((groups, per_group * pairs, 128), full),
            pltpu.VMEM((3, 2, per_group) + grid, half),
            pltpu.VMEM((2, per_group) + grid, half),
            pltpu.VMEM((3, pairs, width, size), half),
            pltpu.VMEM((per_group, 3, 3, size, size), full),
            pltpu.VMEM((3, 3, size, size), full),
            pltpu.VMEM((width, size), full),
            pltpu.VMEM((per_group, 3, 2, pairs, size, width), full),
            pltpu.VMEM((2, per_group, pairs, 2, size, width), half),
            pltpu.VMEM((2, per_group, pairs, 2, size, width), half),
            pltpu.VMEM((3, per_group) + grid, half),
            dma((2,)),
            dma((2,)),
            dma((4, per_group)),
            dma((4, per_group)),
            dma((2, 2, per_group)),
            dma((2, 2, per_group)),
            dma((2, per_group, pairs)),
            dma((2, per_group, pairs)),
            dma((3, per_group)),
            dma((3,)),
        ],
        compiler_params=pltpu.CompilerParams(
            collective_id=0, has_side_effects=True, vmem_limit_bytes=48 * 2**20
        ),
        name="tile_attention_backward",
    )(window, *(x.reshape(split) for x in (key, value, query, grad_out, attn_out)))
    return tuple(x.reshape(query.shape) for x in outs)


def solution(mesh):
    in_specs = (
        P("frame", "head", None),
        P("frame", "head", None),
        P("frame", "head", None),
        P("frame", "head", None),
        P("frame", "head", None),
        P(),
    )
    out_specs = (P("frame", "head", None), P("frame", "head", None), P("frame", "head", None))
    return jax.shard_map(
        on_device, mesh=mesh, in_specs=in_specs, out_specs=out_specs, check_vma=False
    )
```

```python
import functools

import jax
import jax.numpy as jnp
from jax import lax
from jax.experimental import pallas as pl
from jax.experimental.pallas import tpu as pltpu
from jax.sharding import PartitionSpec as P

COLS = 64
TILE = 8
MESH = pl.DeviceIdType.MESH
FAR = -1e30
K, V, Q, G = range(4)


def dot(left, right):
    return jnp.dot(left, right, preferred_element_type=jnp.float32)


def dot_nt(left, right):
    return lax.dot_general(left, right, (((1,), (1,)), ((), ())), preferred_element_type=jnp.float32)


def kernel(
    heads,
    groups,
    frames,
    window_hbm,
    k_ref,
    v_ref,
    q_ref,
    g_ref,
    o_ref,
    dq_ref,
    dk_ref,
    dv_ref,
    g_own,
    o_own,
    delta_out,
    delta_in,
    kv,
    qg,
    k_turned,
    bias,
    scores,
    dq_turned,
    acc,
    parts,
    back,
    zout,
    window_ref,
    own_sems,
    delta_sems,
    zin_send,
    zin_recv,
    halo_send,
    halo_recv,
    back_send,
    back_recv,
    zout_send,
    zout_recv,
):
    per_group = heads // groups
    width = kv.shape[-1]
    scale = width**-0.5
    me = lax.axis_index("head")
    here = lax.axis_index("frame")
    spots = frames // 2
    low, spot = here // spots, lax.rem(here, spots)
    high, core = me // 2, lax.rem(me, 2)
    frame = core * spots + spot
    group = high * 2 + low
    same = core == low
    pairs = kv.shape[5]
    size = groups * kv.shape[4] * kv.shape[6]

    def worker(g):
        return (g // 2 * 2 + low, lax.rem(g, 2) * spots + spot)

    def neighbour(f):
        return (high * 2 + f // spots, low * spots + lax.rem(f, spots))

    up = neighbour(lax.rem(frame + 1, frames))
    down = neighbour(lax.rem(frame + frames - 1, frames))

    own = [
        pltpu.make_async_copy(g_ref, g_own, own_sems.at[0]),
        pltpu.make_async_copy(o_ref, o_own, own_sems.at[1]),
        pltpu.make_async_copy(window_hbm, window_ref, own_sems.at[2]),
    ]
    for copy in own:
        copy.start()

    barrier = pltpu.get_barrier_semaphore()

    @pl.when(jnp.logical_not(same))
    def _():
        pl.semaphore_signal(barrier, 1, device_id=worker(group), device_id_type=MESH)

    for step in range(1, groups):
        pl.semaphore_signal(
            barrier, 1, device_id=worker(lax.rem(group + step, groups)), device_id_type=MESH
        )
    for i in range(groups // 2):
        pl.semaphore_signal(barrier, 1, device_id=(2 * i + 1 - low, frame), device_id_type=MESH)
    for other in (up, down):
        pl.semaphore_signal(barrier, 1, device_id=other, device_id_type=MESH)
    pl.semaphore_wait(barrier, groups - 1 + groups // 2 + 2 + jnp.where(same, 0, 1))

    def landing(array, head):
        return kv.at[0, array, head] if array < 2 else qg.at[array - 2, head]

    def move(step, src, dst, send, recv, to):
        def remote():
            pltpu.make_async_remote_copy(
                src_ref=src, dst_ref=dst, send_sem=send, recv_sem=recv, device_id=to, device_id_type=MESH
            ).start()

        if step > 0:
            remote()
        else:
            pl.when(jnp.logical_not(same))(remote)

            @pl.when(same)
            def _():
                pltpu.make_async_copy(src, dst, recv).start()

    def wait_sent(ref, sem):
        rest = ref.at[1:groups]
        pltpu.make_async_copy(rest, rest, sem).wait()

        @pl.when(jnp.logical_not(same))
        def _():
            pltpu.make_async_copy(ref.at[0], ref.at[0], sem).wait()

    def send_in(array, head):
        ref = (k_ref, v_ref, q_ref, g_ref)[array]
        for step in range(groups):
            to = lax.rem(group + step, groups)
            column = pl.multiple_of((to * per_group + head) * width, width)
            move(
                step,
                ref.at[:, :, :, pl.ds(column, width)],
                landing(array, head).at[me],
                zin_send.at[array, head],
                zin_recv.at[array, head],
                worker(to),
            )

    def arrived(array, head):
        ref = landing(array, head)
        pltpu.make_async_copy(ref, ref, zin_recv.at[array, head]).wait()

    for array in (K, V, Q):
        send_in(array, 0)

    for copy in own:
        copy.wait()
    lane = lax.broadcasted_iota(jnp.int32, (1, 128), 1)
    place = lax.rem(me, 4) * 32
    for h in range(heads):
        cols = slice(h * width, (h + 1) * width)
        product = g_own[:, :, :, cols].astype(jnp.float32) * o_own[:, :, :, cols].astype(jnp.float32)
        turned = product.reshape(128, width).T
        row = jnp.sum(turned, axis=0, keepdims=True)
        for m in range(pairs):
            first = pltpu.roll(row, lax.rem(place + 128 - m * 16, 128), 1)
            second = pltpu.roll(row, lax.rem(place + 16 + 64 - m * 16, 128), 1)
            mine = lane - place
            placed = jnp.where(
                (mine >= 0) & (mine < 16),
                first,
                jnp.where((mine >= 16) & (mine < 32), second, 0.0),
            )
            at = (h % per_group) * pairs + m
            delta_out[h // per_group, at : at + 1, :] = placed
    for step in range(groups):
        to = lax.rem(group + step, groups)
        move(step, delta_out.at[to], delta_in.at[me], delta_sems.at[0], delta_sems.at[1], worker(to))

    k_at = lax.broadcasted_iota(jnp.int32, (size, size), 0)
    q_at = lax.broadcasted_iota(jnp.int32, (size, size), 1)
    row_gap = jnp.abs(k_at // (size // 2) - q_at // (size // 2))
    for head in range(per_group):
        reach_f = window_ref[0, group * per_group + head]
        reach_h = window_ref[1, group * per_group + head]
        reach_w = window_ref[2, group * per_group + head]
        below = jnp.where((reach_f >= 1) & (frame >= 1), 0.0, FAR)
        above = jnp.where((reach_f >= 1) & (frame < frames - 1), 0.0, FAR)
        for gap in (-1, 0, 1):
            col_gap = jnp.abs(2 * gap + (k_at % 16) // 8 - (q_at % 16) // 8)
            near = jnp.where((row_gap <= reach_h) & (col_gap <= reach_w), 0.0, FAR)
            bias[head, 0, gap + 1] = near
            bias[head, 1, gap + 1] = near + below
            bias[head, 2, gap + 1] = near + above

    def halo(array, head, side):
        return pltpu.make_async_remote_copy(
            src_ref=kv.at[0, array, head],
            dst_ref=kv.at[1 + side, array, head],
            send_sem=halo_send.at[side, array, head],
            recv_sem=halo_recv.at[side, array, head],
            device_id=(up, down)[side],
            device_id_type=MESH,
        )

    def send_halo(array, head):
        arrived(array, head)
        for side in range(2):
            halo(array, head, side).start()

    def part_back(head, n, side):
        return pltpu.make_async_remote_copy(
            src_ref=parts.at[side, head, n],
            dst_ref=back.at[side, head, n],
            send_sem=back_send.at[side, head, n],
            recv_sem=back_recv.at[side, head, n],
            device_id=(down, up)[side],
            device_id_type=MESH,
        )

    outs = (dq_ref, dk_ref, dv_ref)

    def send_out(array, head, first, count):
        for step in range(groups):
            to = lax.rem(me + step, groups)
            column = pl.multiple_of((group * per_group + head) * width, width)
            move(
                step,
                zout.at[array, head, to, :, first : first + count],
                outs[array].at[:, first : first + count, :, pl.ds(column, width)],
                zout_send.at[array, head],
                zout_recv.at[array],
                (to, frame),
            )

    def block(ref, n):
        return ref[:, :, n].reshape(size, width)

    def turn(head, o):
        for n in range(pairs):
            k_turned[o, n] = block(kv.at[o, K, head], n).T

    def compute(head, pieces, leaving, after):
        for m in range(pairs):
            near = [n for n in (m - 1, m, m + 1) if 0 <= n < pairs]
            queries = block(qg.at[0, head], m)
            grads = block(qg.at[1, head], m)
            at = head * pairs + m
            halves = [
                sum(delta_in[s, at : at + 1, :] for s in range(half * 4, half * 4 + 4)) for half in range(2)
            ]
            delta = jnp.concatenate(halves, axis=1)

            def score(o, top):
                for n in near:
                    raw = dot_nt(block(kv.at[o, K, head], n), queries)
                    masked = raw * scale + bias[head, o, n - m + 1]
                    scores[o, n - m + 1] = masked
                    top = jnp.maximum(top, jnp.max(masked.reshape(size // 8, 8, size), axis=0))
                return top

            top = lax.fori_loop(0, 3, score, jnp.full((8, size), FAR, jnp.float32))
            top = jnp.max(top, axis=0, keepdims=True)

            def weight(o, total):
                for n in near:
                    e = jnp.exp(scores[o, n - m + 1] - top)
                    scores[o, n - m + 1] = e
                    total = total + jnp.sum(e.reshape(size // 8, 8, size), axis=0)
                return total

            total = lax.fori_loop(0, 3, weight, jnp.zeros((8, size), jnp.float32))
            inverse = 1.0 / jnp.sum(total, axis=0, keepdims=True)
            dq_turned[...] = jnp.zeros_like(dq_turned)

            def backward(o, nothing):
                for n in near:
                    prob = scores[o, n - m + 1] * inverse
                    prob_grad = dot_nt(block(kv.at[o, V, head], n), grads)
                    score_grad = (prob * (prob_grad - delta)).astype(jnp.bfloat16)
                    key_part = dot(score_grad, queries)
                    value_part = dot(prob.astype(jnp.bfloat16), grads)
                    if m == max(n - 1, 0):
                        acc[head, o, 0, n] = key_part
                        acc[head, o, 1, n] = value_part
                    else:
                        acc[head, o, 0, n] += key_part
                        acc[head, o, 1, n] += value_part
                    dq_turned[...] += dot(k_turned[o, n], score_grad)
                return nothing

            lax.fori_loop(0, 3, backward, 0)
            zout[0, head, :, :, m] = (
                (dq_turned[...] * scale).T.astype(jnp.bfloat16).reshape(zout.shape[2], zout.shape[3], 16, width)
            )
            after(m)
            for n in leaving[m]:
                for side in range(2):
                    parts[side, head, n, 0] = (acc[head, 1 + side, 0, n] * scale).astype(jnp.bfloat16)
                    parts[side, head, n, 1] = acc[head, 1 + side, 1, n].astype(jnp.bfloat16)
                    part_back(head, n, side).start()
            step = pairs // pieces
            if (m + 1) % step == 0:
                send_out(0, head, m + 1 - step, step)

    def finish(head, first, count):
        for n in range(first, first + count):
            for side in range(2):
                part_back(head, n, side).wait_recv()
            for array in range(2):
                mine = acc[head, 0, array, n]
                if array == 0:
                    mine = mine * scale
                whole = mine + back[0, head, n, array].astype(jnp.float32) + back[1, head, n, array].astype(jnp.float32)
                zout[1 + array, head, :, :, n] = whole.astype(jnp.bfloat16).reshape(
                    zout.shape[2], zout.shape[3], 16, width
                )
        for array in range(2):
            send_out(1 + array, head, first, count)

    def halo_arrived(array, head):
        for side in range(2):
            halo(array, head, side).wait_recv()

    half = pairs // 2
    send_halo(K, 0)
    send_in(G, 0)
    turn(0, 0)
    send_halo(V, 0)
    send_in(K, 1)
    arrived(Q, 0)
    send_in(V, 1)
    halo_arrived(K, 0)
    turn(0, 1)
    turn(0, 2)
    pltpu.make_async_copy(delta_in, delta_in, delta_sems.at[1]).wait()
    arrived(G, 0)
    send_in(Q, 1)
    halo_arrived(V, 0)

    def during_first(m):
        if m == 1:
            send_halo(K, 1)
            send_in(G, 1)
        elif m == 2:
            send_halo(V, 1)

    compute(0, 1, ((), (), (0, 1), (2, 3)), during_first)
    turn(1, 0)
    halo_arrived(K, 1)
    turn(1, 1)
    turn(1, 2)
    arrived(Q, 1)
    arrived(G, 1)
    halo_arrived(V, 1)

    def during_second(m):
        if m < 2:
            finish(0, m * half, half)

    compute(1, 2, ((), (0,), (1,), (2, 3)), during_second)
    finish(1, 0, half)
    finish(1, half, half)

    for array in range(3):
        pltpu.make_async_copy(outs[array], outs[array], zout_recv.at[array]).wait()
    for head in range(per_group):
        for array in range(3):
            wait_sent(zout.at[array, head], zout_send.at[array, head])
        for array in (K, V, Q, G):
            wait_sent(landing(array, head), zin_send.at[array, head])
        for side in range(2):
            for array in (K, V):
                halo(array, head, side).wait_send()
            for n in range(pairs):
                part_back(head, n, side).wait_send()
    wait_sent(delta_out, delta_sems.at[0])


def settle(*refs):
    ins, outs, held, sems = refs[:3], refs[3:6], refs[6], refs[7]
    fetched = [pltpu.make_async_copy(ins[i], held.at[i], sems.at[0, i]) for i in range(3)]
    stored = [pltpu.make_async_copy(held.at[i], outs[i], sems.at[1, i]) for i in range(3)]
    for copy in fetched:
        copy.start()
    for i in range(3):
        fetched[i].wait()
        stored[i].start()
    for copy in stored:
        copy.wait()


def on_device(query, key, value, grad_out, attn_out, window):
    heads = window.shape[0]
    groups = lax.axis_size("head")
    frames = lax.axis_size("frame")
    tokens = query.shape[1]
    width = query.shape[2] // heads
    per_group = heads // groups
    rows = tokens // COLS
    pairs = COLS // (2 * TILE)
    split = (rows, pairs, 2 * TILE, query.shape[2])
    size = groups * rows * 2 * TILE
    dma = pltpu.SemaphoreType.DMA
    half = jnp.bfloat16
    full = jnp.float32
    in_hbm = pl.BlockSpec(memory_space=pltpu.HBM)
    grid = (groups, rows, pairs, 2 * TILE, width)
    outs = pl.pallas_call(
        functools.partial(kernel, heads, groups, frames),
        out_shape=[jax.ShapeDtypeStruct(split, half)] * 3,
        in_specs=[in_hbm] * 6,
        out_specs=[in_hbm] * 3,
        scratch_shapes=[
            pltpu.VMEM(split, half),
            pltpu.VMEM(split, half),
            pltpu.VMEM((groups, per_group * pairs, 128), full),
            pltpu.VMEM((groups, per_group * pairs, 128), full),
            pltpu.VMEM((3, 2, per_group) + grid, half),
            pltpu.VMEM((2, per_group) + grid, half),
            pltpu.VMEM((3, pairs, width, size), half),
            pltpu.VMEM((per_group, 3, 3, size, size), full),
            pltpu.VMEM((3, 3, size, size), full),
            pltpu.VMEM((width, size), full),
            pltpu.VMEM((per_group, 3, 2, pairs, size, width), full),
            pltpu.VMEM((2, per_group, pairs, 2, size, width), half),
            pltpu.VMEM((2, per_group, pairs, 2, size, width), half),
            pltpu.VMEM((3, per_group) + grid, half),
            pltpu.SMEM((window.shape[1], heads), jnp.int32),
            dma((3,)),
            dma((2,)),
            dma((4, per_group)),
            dma((4, per_group)),
            dma((2, 2, per_group)),
            dma((2, 2, per_group)),
            dma((2, per_group, pairs)),
            dma((2, per_group, pairs)),
            dma((3, per_group)),
            dma((3,)),
        ],
        compiler_params=pltpu.CompilerParams(
            collective_id=0, has_side_effects=True, vmem_limit_bytes=62 * 2**20
        ),
        name="tile_attention_backward",
    )(window.T, *(x.reshape(split) for x in (key, value, query, grad_out, attn_out)))
    outs = pl.pallas_call(
        settle,
        out_shape=[jax.ShapeDtypeStruct(split, half)] * 3,
        in_specs=[in_hbm] * 3,
        out_specs=[in_hbm] * 3,
        scratch_shapes=[pltpu.VMEM((3,) + split, half), dma((2, 3))],
        compiler_params=pltpu.CompilerParams(vmem_limit_bytes=62 * 2**20),
        name="settle",
    )(*outs)
    return tuple(x.reshape(query.shape) for x in outs)


def solution(mesh):
    in_specs = (
        P("frame", "head", None),
        P("frame", "head", None),
        P("frame", "head", None),
        P("frame", "head", None),
        P("frame", "head", None),
        P(),
    )
    out_specs = (P("frame", "head", None), P("frame", "head", None), P("frame", "head", None))
    return jax.shard_map(
        on_device, mesh=mesh, in_specs=in_specs, out_specs=out_specs, check_vma=False
    )
```

```python
import functools

import jax
import jax.numpy as jnp
from jax import lax
from jax.experimental import pallas as pl
from jax.experimental.pallas import tpu as pltpu
from jax.sharding import PartitionSpec as P

COLS = 64
TILE = 8
MESH = pl.DeviceIdType.MESH
FAR = -1e30
K, V, Q, G = range(4)


def dot(left, right):
    return jnp.dot(left, right, preferred_element_type=jnp.float32)


def dot_nt(left, right):
    return lax.dot_general(left, right, (((1,), (1,)), ((), ())), preferred_element_type=jnp.float32)


def kernel(
    heads,
    groups,
    frames,
    window_hbm,
    k_ref,
    v_ref,
    q_ref,
    g_ref,
    o_ref,
    dq_ref,
    dk_ref,
    dv_ref,
    g_own,
    o_own,
    delta_out,
    delta_in,
    kv,
    qg,
    k_turned,
    bias,
    scores,
    dq_turned,
    acc,
    parts,
    back,
    zout,
    window_ref,
    own_sems,
    delta_sems,
    zin_send,
    zin_recv,
    halo_send,
    halo_recv,
    back_send,
    back_recv,
    zout_send,
    zout_recv,
    met,
):
    per_group = heads // groups
    width = kv.shape[-1]
    scale = width**-0.5
    me = lax.axis_index("head")
    here = lax.axis_index("frame")
    spots = frames // 2
    low, spot = here // spots, lax.rem(here, spots)
    high, core = me // 2, lax.rem(me, 2)
    frame = core * spots + spot
    group = high * 2 + low
    same = core == low
    pairs = kv.shape[5]
    size = groups * kv.shape[4] * kv.shape[6]

    def worker(g):
        return (g // 2 * 2 + low, lax.rem(g, 2) * spots + spot)

    def neighbour(f):
        return (high * 2 + f // spots, low * spots + lax.rem(f, spots))

    up = neighbour(lax.rem(frame + 1, frames))
    down = neighbour(lax.rem(frame + frames - 1, frames))

    barrier = pltpu.get_barrier_semaphore()

    @pl.when(jnp.logical_not(same))
    def _():
        pl.semaphore_signal(barrier, 1, device_id=worker(group), device_id_type=MESH)

    for step in range(1, groups):
        pl.semaphore_signal(
            barrier, 1, device_id=worker(lax.rem(group + step, groups)), device_id_type=MESH
        )
    for i in range(groups // 2):
        pl.semaphore_signal(barrier, 1, device_id=(2 * i + 1 - low, frame), device_id_type=MESH)
    at_end = spot == spots - 1
    at_start = spot == 0

    def signal(condition, sem, other):
        @pl.when(condition)
        def _():
            pl.semaphore_signal(sem, 1, device_id=other, device_id_type=MESH)

    signal(jnp.logical_not(at_end), barrier, up)
    signal(at_start, barrier, down)
    own = [
        pltpu.make_async_copy(g_ref, g_own, own_sems.at[0]),
        pltpu.make_async_copy(o_ref, o_own, own_sems.at[1]),
        pltpu.make_async_copy(window_hbm, window_ref, own_sems.at[2]),
    ]
    for copy in own:
        copy.start()

    count = groups - 1 + groups // 2 + jnp.where(same, 0, 1)
    pl.semaphore_wait(barrier, count + jnp.where(at_start, 0, 1) + jnp.where(at_end, 1, 0))
    signal(jnp.logical_not(at_start), met.at[0], down)
    signal(at_end, met.at[1], up)

    def landing(array, head):
        return kv.at[0, array, head] if array < 2 else qg.at[array - 2, head]

    def move(step, src, dst, send, recv, to):
        def remote():
            pltpu.make_async_remote_copy(
                src_ref=src, dst_ref=dst, send_sem=send, recv_sem=recv, device_id=to, device_id_type=MESH
            ).start()

        if step > 0:
            remote()
        else:
            pl.when(jnp.logical_not(same))(remote)

            @pl.when(same)
            def _():
                pltpu.make_async_copy(src, dst, recv).start()

    def wait_sent(ref, sem):
        rest = ref.at[1:groups]
        pltpu.make_async_copy(rest, rest, sem).wait()

        @pl.when(jnp.logical_not(same))
        def _():
            pltpu.make_async_copy(ref.at[0], ref.at[0], sem).wait()

    def send_in(array, head):
        ref = (k_ref, v_ref, q_ref, g_ref)[array]
        for step in range(groups):
            to = lax.rem(group + step, groups)
            column = pl.multiple_of((to * per_group + head) * width, width)
            move(
                step,
                ref.at[:, :, :, pl.ds(column, width)],
                landing(array, head).at[me],
                zin_send.at[array, head],
                zin_recv.at[array, head],
                worker(to),
            )

    def arrived(array, head):
        ref = landing(array, head)
        pltpu.make_async_copy(ref, ref, zin_recv.at[array, head]).wait()

    for array in (K, V, Q):
        send_in(array, 0)

    for copy in own:
        copy.wait()
    lane = lax.broadcasted_iota(jnp.int32, (1, 128), 1)
    place = lax.rem(me, 4) * 32
    for h in range(heads):
        cols = slice(h * width, (h + 1) * width)
        product = g_own[:, :, :, cols].astype(jnp.float32) * o_own[:, :, :, cols].astype(jnp.float32)
        turned = product.reshape(128, width).T
        row = jnp.sum(turned, axis=0, keepdims=True)
        for m in range(pairs):
            first = pltpu.roll(row, lax.rem(place + 128 - m * 16, 128), 1)
            second = pltpu.roll(row, lax.rem(place + 16 + 64 - m * 16, 128), 1)
            mine = lane - place
            placed = jnp.where(
                (mine >= 0) & (mine < 16),
                first,
                jnp.where((mine >= 16) & (mine < 32), second, 0.0),
            )
            at = (h % per_group) * pairs + m
            delta_out[h // per_group, at : at + 1, :] = placed
    for step in range(groups):
        to = lax.rem(group + step, groups)
        move(step, delta_out.at[to], delta_in.at[me], delta_sems.at[0], delta_sems.at[1], worker(to))

    k_at = lax.broadcasted_iota(jnp.int32, (size, size), 0)
    q_at = lax.broadcasted_iota(jnp.int32, (size, size), 1)
    row_gap = jnp.abs(k_at // (size // 2) - q_at // (size // 2))
    for head in range(per_group):
        reach_f = window_ref[0, group * per_group + head]
        reach_h = window_ref[1, group * per_group + head]
        reach_w = window_ref[2, group * per_group + head]
        below = jnp.where((reach_f >= 1) & (frame >= 1), 0.0, FAR)
        above = jnp.where((reach_f >= 1) & (frame < frames - 1), 0.0, FAR)
        for gap in (-1, 0, 1):
            col_gap = jnp.abs(2 * gap + (k_at % 16) // 8 - (q_at % 16) // 8)
            near = jnp.where((row_gap <= reach_h) & (col_gap <= reach_w), 0.0, FAR)
            bias[head, 0, gap + 1] = near
            bias[head, 1, gap + 1] = near + below
            bias[head, 2, gap + 1] = near + above

    def halo(array, head, side):
        return pltpu.make_async_remote_copy(
            src_ref=kv.at[0, array, head],
            dst_ref=kv.at[1 + side, array, head],
            send_sem=halo_send.at[side, array, head],
            recv_sem=halo_recv.at[side, array, head],
            device_id=(up, down)[side],
            device_id_type=MESH,
        )

    def send_halo(array, head):
        arrived(array, head)
        for side in range(2):
            halo(array, head, side).start()

    def part_back(head, n, side):
        return pltpu.make_async_remote_copy(
            src_ref=parts.at[side, head, n],
            dst_ref=back.at[side, head, n],
            send_sem=back_send.at[side, head, n],
            recv_sem=back_recv.at[side, head, n],
            device_id=(down, up)[side],
            device_id_type=MESH,
        )

    outs = (dq_ref, dk_ref, dv_ref)

    def send_out(array, head, first, count):
        for step in range(groups):
            to = lax.rem(me + step, groups)
            column = pl.multiple_of((group * per_group + head) * width, width)
            move(
                step,
                zout.at[array, head, to, :, first : first + count],
                outs[array].at[:, first : first + count, :, pl.ds(column, width)],
                zout_send.at[array, head],
                zout_recv.at[array],
                (to, frame),
            )

    def block(ref, n):
        return ref[:, :, n].reshape(size, width)

    def turn(head, o):
        for n in range(pairs):
            k_turned[o, n] = block(kv.at[o, K, head], n).T

    def compute(head, pieces, leaving, after):
        for m in range(pairs):
            near = [n for n in (m - 1, m, m + 1) if 0 <= n < pairs]
            queries = block(qg.at[0, head], m)
            grads = block(qg.at[1, head], m)
            at = head * pairs + m
            halves = [
                sum(delta_in[s, at : at + 1, :] for s in range(half * 4, half * 4 + 4)) for half in range(2)
            ]
            delta = jnp.concatenate(halves, axis=1)

            def score(o, top):
                for n in near:
                    raw = dot_nt(block(kv.at[o, K, head], n), queries)
                    masked = raw * scale + bias[head, o, n - m + 1]
                    scores[o, n - m + 1] = masked
                    top = jnp.maximum(top, jnp.max(masked.reshape(size // 8, 8, size), axis=0))
                return top

            top = lax.fori_loop(0, 3, score, jnp.full((8, size), FAR, jnp.float32), unroll=True)
            top = jnp.max(top, axis=0, keepdims=True)

            def weight(o, total):
                for n in near:
                    e = jnp.exp(scores[o, n - m + 1] - top)
                    scores[o, n - m + 1] = e
                    total = total + jnp.sum(e.reshape(size // 8, 8, size), axis=0)
                return total

            total = lax.fori_loop(0, 3, weight, jnp.zeros((8, size), jnp.float32), unroll=True)
            inverse = 1.0 / jnp.sum(total, axis=0, keepdims=True)
            dq_turned[...] = jnp.zeros_like(dq_turned)

            def backward(o, nothing):
                for n in near:
                    prob = scores[o, n - m + 1] * inverse
                    prob_grad = dot_nt(block(kv.at[o, V, head], n), grads)
                    score_grad = (prob * (prob_grad - delta)).astype(jnp.bfloat16)
                    key_part = dot(score_grad, queries)
                    value_part = dot(prob.astype(jnp.bfloat16), grads)
                    if m == max(n - 1, 0):
                        acc[head, o, 0, n] = key_part
                        acc[head, o, 1, n] = value_part
                    else:
                        acc[head, o, 0, n] += key_part
                        acc[head, o, 1, n] += value_part
                    dq_turned[...] += dot(k_turned[o, n], score_grad)
                return nothing

            lax.fori_loop(0, 3, backward, 0, unroll=True)
            zout[0, head, :, :, m] = (
                (dq_turned[...] * scale).T.astype(jnp.bfloat16).reshape(zout.shape[2], zout.shape[3], 16, width)
            )
            after(m)
            for n in leaving[m]:
                for side in range(2):
                    parts[side, head, n, 0] = (acc[head, 1 + side, 0, n] * scale).astype(jnp.bfloat16)
                    parts[side, head, n, 1] = acc[head, 1 + side, 1, n].astype(jnp.bfloat16)
                    part_back(head, n, side).start()
            step = pairs // pieces
            if (m + 1) % step == 0:
                send_out(0, head, m + 1 - step, step)

    def finish(head, first, count):
        for n in range(first, first + count):
            for side in range(2):
                part_back(head, n, side).wait_recv()
            for array in range(2):
                mine = acc[head, 0, array, n]
                if array == 0:
                    mine = mine * scale
                whole = mine + back[0, head, n, array].astype(jnp.float32) + back[1, head, n, array].astype(jnp.float32)
                zout[1 + array, head, :, :, n] = whole.astype(jnp.bfloat16).reshape(
                    zout.shape[2], zout.shape[3], 16, width
                )
        for array in range(2):
            send_out(1 + array, head, first, count)

    def halo_arrived(array, head):
        for side in range(2):
            halo(array, head, side).wait_recv()

    half = pairs // 2

    @pl.when(jnp.logical_not(at_end))
    def _():
        pl.semaphore_wait(met.at[0], 1)

    @pl.when(at_start)
    def _():
        pl.semaphore_wait(met.at[1], 1)

    send_halo(K, 0)
    send_in(G, 0)
    turn(0, 0)
    send_halo(V, 0)
    send_in(K, 1)
    arrived(Q, 0)
    send_in(V, 1)
    halo_arrived(K, 0)
    turn(0, 1)
    turn(0, 2)
    pltpu.make_async_copy(delta_in, delta_in, delta_sems.at[1]).wait()
    arrived(G, 0)
    send_in(Q, 1)
    halo_arrived(V, 0)

    def during_first(m):
        if m == 1:
            send_halo(K, 1)
            send_in(G, 1)
        elif m == 2:
            send_halo(V, 1)

    compute(0, 1, ((), (), (0, 1), (2, 3)), during_first)
    turn(1, 0)
    halo_arrived(K, 1)
    turn(1, 1)
    turn(1, 2)
    arrived(Q, 1)
    arrived(G, 1)
    halo_arrived(V, 1)

    def during_second(m):
        if m < 2:
            finish(0, m * half, half)

    compute(1, 2, ((), (0,), (1,), (2, 3)), during_second)
    finish(1, 0, half)
    finish(1, half, half)

    for array in range(3):
        pltpu.make_async_copy(outs[array], outs[array], zout_recv.at[array]).wait()
    for head in range(per_group):
        for array in range(3):
            wait_sent(zout.at[array, head], zout_send.at[array, head])
        for array in (K, V, Q, G):
            wait_sent(landing(array, head), zin_send.at[array, head])
        for side in range(2):
            for array in (K, V):
                halo(array, head, side).wait_send()
            for n in range(pairs):
                part_back(head, n, side).wait_send()
    wait_sent(delta_out, delta_sems.at[0])


def settle(*refs):
    copies = [pltpu.make_async_copy(refs[i], refs[3 + i], refs[6].at[i]) for i in range(3)]
    for copy in copies:
        copy.start()
    for copy in copies:
        copy.wait()


def on_device(query, key, value, grad_out, attn_out, window):
    heads = window.shape[0]
    groups = lax.axis_size("head")
    frames = lax.axis_size("frame")
    tokens = query.shape[1]
    width = query.shape[2] // heads
    per_group = heads // groups
    rows = tokens // COLS
    pairs = COLS // (2 * TILE)
    split = (rows, pairs, 2 * TILE, query.shape[2])
    size = groups * rows * 2 * TILE
    dma = pltpu.SemaphoreType.DMA
    half = jnp.bfloat16
    full = jnp.float32
    in_hbm = pl.BlockSpec(memory_space=pltpu.HBM)
    grid = (groups, rows, pairs, 2 * TILE, width)
    outs = pl.pallas_call(
        functools.partial(kernel, heads, groups, frames),
        out_shape=[pltpu.VMEM(split, half)] * 3,
        in_specs=[in_hbm] * 6,
        out_specs=[pl.BlockSpec(memory_space=pltpu.VMEM)] * 3,
        scratch_shapes=[
            pltpu.VMEM(split, half),
            pltpu.VMEM(split, half),
            pltpu.VMEM((groups, per_group * pairs, 128), full),
            pltpu.VMEM((groups, per_group * pairs, 128), full),
            pltpu.VMEM((3, 2, per_group) + grid, half),
            pltpu.VMEM((2, per_group) + grid, half),
            pltpu.VMEM((3, pairs, width, size), half),
            pltpu.VMEM((per_group, 3, 3, size, size), full),
            pltpu.VMEM((3, 3, size, size), full),
            pltpu.VMEM((width, size), full),
            pltpu.VMEM((per_group, 3, 2, pairs, size, width), full),
            pltpu.VMEM((2, per_group, pairs, 2, size, width), half),
            pltpu.VMEM((2, per_group, pairs, 2, size, width), half),
            pltpu.VMEM((3, per_group) + grid, half),
            pltpu.SMEM((window.shape[1], heads), jnp.int32),
            dma((3,)),
            dma((2,)),
            dma((4, per_group)),
            dma((4, per_group)),
            dma((2, 2, per_group)),
            dma((2, 2, per_group)),
            dma((2, per_group, pairs)),
            dma((2, per_group, pairs)),
            dma((3, per_group)),
            dma((3,)),
            pltpu.SemaphoreType.REGULAR((2,)),
        ],
        compiler_params=pltpu.CompilerParams(
            collective_id=0, has_side_effects=True, vmem_limit_bytes=56 * 2**20
        ),
        name="tile_attention_backward",
    )(window.T, *(x.reshape(split) for x in (key, value, query, grad_out, attn_out)))
    outs = pl.pallas_call(
        settle,
        out_shape=[jax.ShapeDtypeStruct(split, half)] * 3,
        in_specs=[pl.BlockSpec(memory_space=pltpu.VMEM)] * 3,
        out_specs=[in_hbm] * 3,
        scratch_shapes=[dma((3,))],
        compiler_params=pltpu.CompilerParams(vmem_limit_bytes=8 * 2**20),
        name="settle",
    )(*outs)
    return tuple(x.reshape(query.shape) for x in outs)


def solution(mesh):
    in_specs = (
        P("frame", "head", None),
        P("frame", "head", None),
        P("frame", "head", None),
        P("frame", "head", None),
        P("frame", "head", None),
        P(),
    )
    out_specs = (P("frame", "head", None), P("frame", "head", None), P("frame", "head", None))
    return jax.shard_map(
        on_device, mesh=mesh, in_specs=in_specs, out_specs=out_specs, check_vma=False
    )
```

```python
import functools

import jax
import jax.numpy as jnp
from jax import lax
from jax.experimental import pallas as pl
from jax.experimental.pallas import tpu as pltpu
from jax.sharding import PartitionSpec as P

COLS = 64
TILE = 8
MESH = pl.DeviceIdType.MESH
FAR = -1e30
K, V, Q, G = range(4)


def dot(left, right):
    return jnp.dot(left, right, preferred_element_type=jnp.float32)


def dot_nt(left, right):
    return lax.dot_general(left, right, (((1,), (1,)), ((), ())), preferred_element_type=jnp.float32)


def kernel(
    heads,
    groups,
    frames,
    window_hbm,
    k_ref,
    v_ref,
    q_ref,
    g_ref,
    o_ref,
    dq_ref,
    dk_ref,
    dv_ref,
    g_own,
    o_own,
    delta_out,
    delta_in,
    kv,
    qg,
    k_turned,
    bias,
    scores,
    dq_turned,
    acc,
    parts,
    back,
    zout,
    window_ref,
    own_sems,
    delta_sems,
    zin_send,
    zin_recv,
    halo_send,
    halo_recv,
    back_send,
    back_recv,
    zout_send,
    zout_recv,
    met,
):
    per_group = heads // groups
    width = kv.shape[-1]
    scale = width**-0.5
    me = lax.axis_index("head")
    here = lax.axis_index("frame")
    spots = frames // 2
    low, spot = here // spots, lax.rem(here, spots)
    high, core = me // 2, lax.rem(me, 2)
    frame = core * spots + spot
    group = high * 2 + low
    same = core == low
    pairs = kv.shape[5]
    size = groups * kv.shape[4] * kv.shape[6]

    def worker(g):
        return (g // 2 * 2 + low, lax.rem(g, 2) * spots + spot)

    def neighbour(f):
        return (high * 2 + f // spots, low * spots + lax.rem(f, spots))

    up = neighbour(lax.rem(frame + 1, frames))
    down = neighbour(lax.rem(frame + frames - 1, frames))

    barrier = pltpu.get_barrier_semaphore()

    @pl.when(jnp.logical_not(same))
    def _():
        pl.semaphore_signal(barrier, 1, device_id=worker(group), device_id_type=MESH)

    for step in range(1, groups):
        pl.semaphore_signal(
            barrier, 1, device_id=worker(lax.rem(group + step, groups)), device_id_type=MESH
        )
    for i in range(groups // 2):
        pl.semaphore_signal(barrier, 1, device_id=(2 * i + 1 - low, frame), device_id_type=MESH)
    at_end = spot == spots - 1
    at_start = spot == 0

    def signal(condition, sem, other):
        @pl.when(condition)
        def _():
            pl.semaphore_signal(sem, 1, device_id=other, device_id_type=MESH)

    signal(jnp.logical_not(at_end), barrier, up)
    signal(at_start, barrier, down)
    own = [
        pltpu.make_async_copy(g_ref, g_own, own_sems.at[0]),
        pltpu.make_async_copy(o_ref, o_own, own_sems.at[1]),
        pltpu.make_async_copy(window_hbm, window_ref, own_sems.at[2]),
    ]
    for copy in own:
        copy.start()

    count = groups - 1 + groups // 2 + jnp.where(same, 0, 1)
    pl.semaphore_wait(barrier, count + jnp.where(at_start, 0, 1) + jnp.where(at_end, 1, 0))
    signal(jnp.logical_not(at_start), met.at[0], down)
    signal(at_end, met.at[1], up)

    def landing(array, head):
        return kv.at[0, array, head] if array < 2 else qg.at[array - 2, head]

    def move(stays, src, dst, send, recv, to):
        def remote():
            pltpu.make_async_remote_copy(
                src_ref=src, dst_ref=dst, send_sem=send, recv_sem=recv, device_id=to, device_id_type=MESH
            ).start()

        if stays is None:
            remote()
        else:
            pl.when(jnp.logical_not(stays))(remote)

            @pl.when(stays)
            def _():
                pltpu.make_async_copy(src, dst, recv).start()

    def wait_sent(ref, sem):
        rest = ref.at[1:groups]
        pltpu.make_async_copy(rest, rest, sem).wait()

        @pl.when(jnp.logical_not(same))
        def _():
            pltpu.make_async_copy(ref.at[0], ref.at[0], sem).wait()

    def send_in(array, head):
        ref = (k_ref, v_ref, q_ref, g_ref)[array]
        for step in range(groups):
            to = lax.rem(group + step, groups)
            column = pl.multiple_of((to * per_group + head) * width, width)
            move(
                same if step == 0 else None,
                ref.at[:, :, :, pl.ds(column, width)],
                landing(array, head).at[me],
                zin_send.at[array, head],
                zin_recv.at[array, head],
                worker(to),
            )

    def arrived(array, head):
        ref = landing(array, head)
        pltpu.make_async_copy(ref, ref, zin_recv.at[array, head]).wait()

    for array in (K, V, Q):
        send_in(array, 0)

    for copy in own:
        copy.wait()
    lane = lax.broadcasted_iota(jnp.int32, (1, 128), 1)
    place = lax.rem(me, 4) * 32
    for h in range(heads):
        cols = slice(h * width, (h + 1) * width)
        product = g_own[:, :, :, cols].astype(jnp.float32) * o_own[:, :, :, cols].astype(jnp.float32)
        turned = product.reshape(128, width).T
        row = jnp.sum(turned, axis=0, keepdims=True)
        for m in range(pairs):
            first = pltpu.roll(row, lax.rem(place + 128 - m * 16, 128), 1)
            second = pltpu.roll(row, lax.rem(place + 16 + 64 - m * 16, 128), 1)
            mine = lane - place
            placed = jnp.where(
                (mine >= 0) & (mine < 16),
                first,
                jnp.where((mine >= 16) & (mine < 32), second, 0.0),
            )
            at = (h % per_group) * pairs + m
            delta_out[h // per_group, at : at + 1, :] = placed
    for step in range(groups):
        to = lax.rem(group + step, groups)
        move(same if step == 0 else None, delta_out.at[to], delta_in.at[me], delta_sems.at[0], delta_sems.at[1], worker(to))

    k_at = lax.broadcasted_iota(jnp.int32, (size, size), 0)
    q_at = lax.broadcasted_iota(jnp.int32, (size, size), 1)
    row_gap = jnp.abs(k_at // (size // 2) - q_at // (size // 2))
    for head in range(per_group):
        reach_f = window_ref[0, group * per_group + head]
        reach_h = window_ref[1, group * per_group + head]
        reach_w = window_ref[2, group * per_group + head]
        below = jnp.where((reach_f >= 1) & (frame >= 1), 0.0, FAR)
        above = jnp.where((reach_f >= 1) & (frame < frames - 1), 0.0, FAR)
        for gap in (-1, 0, 1):
            col_gap = jnp.abs(2 * gap + (k_at % 16) // 8 - (q_at % 16) // 8)
            near = jnp.where((row_gap <= reach_h) & (col_gap <= reach_w), 0.0, FAR)
            bias[head, 0, gap + 1] = near
            bias[head, 1, gap + 1] = near + below
            bias[head, 2, gap + 1] = near + above

    def halo(array, head, side):
        return pltpu.make_async_remote_copy(
            src_ref=kv.at[0, array, head],
            dst_ref=kv.at[1 + side, array, head],
            send_sem=halo_send.at[side, array, head],
            recv_sem=halo_recv.at[side, array, head],
            device_id=(up, down)[side],
            device_id_type=MESH,
        )

    def send_halo(array, head):
        arrived(array, head)
        for side in range(2):
            halo(array, head, side).start()

    def part_back(head, n, side):
        return pltpu.make_async_remote_copy(
            src_ref=parts.at[side, head, n],
            dst_ref=back.at[side, head, n],
            send_sem=back_send.at[side, head, n],
            recv_sem=back_recv.at[side, head, n],
            device_id=(down, up)[side],
            device_id_type=MESH,
        )

    outs = (dq_ref, dk_ref, dv_ref)

    def send_piece(array, head, first, count, to, stays):
        column = pl.multiple_of((group * per_group + head) * width, width)
        move(
            stays,
            zout.at[array, head, to, :, first : first + count],
            outs[array].at[:, first : first + count, :, pl.ds(column, width)],
            zout_send.at[array, head],
            zout_recv.at[array],
            (to, frame),
        )

    def send_out(array, head, first, count):
        for step in range(groups):
            stays = same if step == 0 else None
            send_piece(array, head, first, count, lax.rem(me + step, groups), stays)

    def send_last(head, first, count):
        targets = [0, 1] + [2 + lax.rem(me + step, groups - 2) for step in range(groups - 2)]
        for to in targets:
            for array in (1, 2):
                send_piece(array, head, first, count, to, same & (me == to))

    def block(ref, n):
        return ref[:, :, n].reshape(size, width)

    def turn(head, o):
        for n in range(pairs):
            k_turned[o, n] = block(kv.at[o, K, head], n).T

    def compute(head, leaving, before, after):
        for m in range(pairs):
            near = [n for n in (m - 1, m, m + 1) if 0 <= n < pairs]
            queries = block(qg.at[0, head], m)
            grads = block(qg.at[1, head], m)
            at = head * pairs + m
            halves = [
                sum(delta_in[s, at : at + 1, :] for s in range(half * 4, half * 4 + 4)) for half in range(2)
            ]
            delta = jnp.concatenate(halves, axis=1)

            def score(o, top):
                for n in near:
                    raw = dot_nt(block(kv.at[o, K, head], n), queries)
                    masked = raw * scale + bias[head, o, n - m + 1]
                    scores[o, n - m + 1] = masked
                    top = jnp.maximum(top, jnp.max(masked.reshape(size // 8, 8, size), axis=0))
                return top

            top = lax.fori_loop(0, 3, score, jnp.full((8, size), FAR, jnp.float32), unroll=True)
            top = jnp.max(top, axis=0, keepdims=True)

            def weight(o, total):
                for n in near:
                    e = jnp.exp(scores[o, n - m + 1] - top)
                    scores[o, n - m + 1] = e
                    total = total + jnp.sum(e.reshape(size // 8, 8, size), axis=0)
                return total

            total = lax.fori_loop(0, 3, weight, jnp.zeros((8, size), jnp.float32), unroll=True)
            inverse = 1.0 / jnp.sum(total, axis=0, keepdims=True)
            dq_turned[...] = jnp.zeros_like(dq_turned)

            def backward(o, nothing):
                for n in near:
                    prob = scores[o, n - m + 1] * inverse
                    prob_grad = dot_nt(block(kv.at[o, V, head], n), grads)
                    score_grad = (prob * (prob_grad - delta)).astype(jnp.bfloat16)
                    key_part = dot(score_grad, queries)
                    value_part = dot(prob.astype(jnp.bfloat16), grads)
                    if m == max(n - 1, 0):
                        acc[head, o, 0, n] = key_part
                        acc[head, o, 1, n] = value_part
                    else:
                        acc[head, o, 0, n] += key_part
                        acc[head, o, 1, n] += value_part
                    dq_turned[...] += dot(k_turned[o, n], score_grad)
                return nothing

            lax.fori_loop(0, 3, backward, 0, unroll=True)
            zout[0, head, :, :, m] = (
                (dq_turned[...] * scale).T.astype(jnp.bfloat16).reshape(zout.shape[2], zout.shape[3], 16, width)
            )
            before(m)
            for n in leaving[m]:
                for side in range(2):
                    parts[side, head, n, 0] = (acc[head, 1 + side, 0, n] * scale).astype(jnp.bfloat16)
                    parts[side, head, n, 1] = acc[head, 1 + side, 1, n].astype(jnp.bfloat16)
                    part_back(head, n, side).start()
            after(m)

    def finish(head, first, count, final=False):
        for n in range(first, first + count):
            for side in range(2):
                part_back(head, n, side).wait_recv()
            for array in range(2):
                mine = acc[head, 0, array, n]
                if array == 0:
                    mine = mine * scale
                whole = mine + back[0, head, n, array].astype(jnp.float32) + back[1, head, n, array].astype(jnp.float32)
                zout[1 + array, head, :, :, n] = whole.astype(jnp.bfloat16).reshape(
                    zout.shape[2], zout.shape[3], 16, width
                )
        if final:
            send_last(head, first, count)
        else:
            for array in range(2):
                send_out(1 + array, head, first, count)

    def halo_arrived(array, head):
        for side in range(2):
            halo(array, head, side).wait_recv()

    half = pairs // 2

    @pl.when(jnp.logical_not(at_end))
    def _():
        pl.semaphore_wait(met.at[0], 1)

    @pl.when(at_start)
    def _():
        pl.semaphore_wait(met.at[1], 1)

    send_halo(K, 0)
    send_in(G, 0)
    turn(0, 0)
    send_halo(V, 0)
    send_in(K, 1)
    arrived(Q, 0)
    send_in(V, 1)
    halo_arrived(K, 0)
    turn(0, 1)
    turn(0, 2)
    pltpu.make_async_copy(delta_in, delta_in, delta_sems.at[1]).wait()
    arrived(G, 0)
    send_in(Q, 1)
    halo_arrived(V, 0)

    def nothing(m):
        pass

    def during_first(m):
        if m == 1:
            send_halo(K, 1)
            send_in(G, 1)
        elif m == 2:
            send_halo(V, 1)

    compute(0, ((), (), (0, 1), (2, 3)), during_first, nothing)
    send_out(0, 0, 0, pairs)
    turn(1, 0)
    halo_arrived(K, 1)
    turn(1, 1)
    turn(1, 2)
    arrived(Q, 1)
    arrived(G, 1)
    halo_arrived(V, 1)

    def during_second(m):
        if m < half:
            send_out(0, 1, m, 1)
        if m == 1:
            finish(0, 0, half)
        elif m == 2:
            finish(0, half, 1)

    compute(1, ((), (0,), (1,), (2, 3)), nothing, during_second)
    finish(0, half + 1, half - 1)
    send_out(0, 1, half, half)
    finish(1, 0, half)
    finish(1, half, half, True)

    for array in range(3):
        pltpu.make_async_copy(outs[array], outs[array], zout_recv.at[array]).wait()
    for head in range(per_group):
        for array in range(3):
            wait_sent(zout.at[array, head], zout_send.at[array, head])
        for array in (K, V, Q, G):
            wait_sent(landing(array, head), zin_send.at[array, head])
        for side in range(2):
            for array in (K, V):
                halo(array, head, side).wait_send()
            for n in range(pairs):
                part_back(head, n, side).wait_send()
    wait_sent(delta_out, delta_sems.at[0])


def settle(*refs):
    copies = [pltpu.make_async_copy(refs[i], refs[3 + i], refs[6].at[i]) for i in range(3)]
    for copy in copies:
        copy.start()
    for copy in copies:
        copy.wait()


def on_device(query, key, value, grad_out, attn_out, window):
    heads = window.shape[0]
    groups = lax.axis_size("head")
    frames = lax.axis_size("frame")
    tokens = query.shape[1]
    width = query.shape[2] // heads
    per_group = heads // groups
    rows = tokens // COLS
    pairs = COLS // (2 * TILE)
    split = (rows, pairs, 2 * TILE, query.shape[2])
    size = groups * rows * 2 * TILE
    dma = pltpu.SemaphoreType.DMA
    half = jnp.bfloat16
    full = jnp.float32
    in_hbm = pl.BlockSpec(memory_space=pltpu.HBM)
    grid = (groups, rows, pairs, 2 * TILE, width)
    outs = pl.pallas_call(
        functools.partial(kernel, heads, groups, frames),
        out_shape=[pltpu.VMEM(split, half)] * 3,
        in_specs=[in_hbm] * 6,
        out_specs=[pl.BlockSpec(memory_space=pltpu.VMEM)] * 3,
        scratch_shapes=[
            pltpu.VMEM(split, half),
            pltpu.VMEM(split, half),
            pltpu.VMEM((groups, per_group * pairs, 128), full),
            pltpu.VMEM((groups, per_group * pairs, 128), full),
            pltpu.VMEM((3, 2, per_group) + grid, half),
            pltpu.VMEM((2, per_group) + grid, half),
            pltpu.VMEM((3, pairs, width, size), half),
            pltpu.VMEM((per_group, 3, 3, size, size), full),
            pltpu.VMEM((3, 3, size, size), full),
            pltpu.VMEM((width, size), full),
            pltpu.VMEM((per_group, 3, 2, pairs, size, width), full),
            pltpu.VMEM((2, per_group, pairs, 2, size, width), half),
            pltpu.VMEM((2, per_group, pairs, 2, size, width), half),
            pltpu.VMEM((3, per_group) + grid, half),
            pltpu.SMEM((window.shape[1], heads), jnp.int32),
            dma((3,)),
            dma((2,)),
            dma((4, per_group)),
            dma((4, per_group)),
            dma((2, 2, per_group)),
            dma((2, 2, per_group)),
            dma((2, per_group, pairs)),
            dma((2, per_group, pairs)),
            dma((3, per_group)),
            dma((3,)),
            pltpu.SemaphoreType.REGULAR((2,)),
        ],
        compiler_params=pltpu.CompilerParams(
            collective_id=0, has_side_effects=True, vmem_limit_bytes=56 * 2**20
        ),
        name="tile_attention_backward",
    )(window.T, *(x.reshape(split) for x in (key, value, query, grad_out, attn_out)))
    outs = pl.pallas_call(
        settle,
        out_shape=[jax.ShapeDtypeStruct(split, half)] * 3,
        in_specs=[pl.BlockSpec(memory_space=pltpu.VMEM)] * 3,
        out_specs=[in_hbm] * 3,
        scratch_shapes=[dma((3,))],
        compiler_params=pltpu.CompilerParams(vmem_limit_bytes=8 * 2**20),
        name="settle",
    )(*outs)
    return tuple(x.reshape(query.shape) for x in outs)


def solution(mesh):
    in_specs = (
        P("frame", "head", None),
        P("frame", "head", None),
        P("frame", "head", None),
        P("frame", "head", None),
        P("frame", "head", None),
        P(),
    )
    out_specs = (P("frame", "head", None), P("frame", "head", None), P("frame", "head", None))
    return jax.shard_map(
        on_device, mesh=mesh, in_specs=in_specs, out_specs=out_specs, check_vma=False
    )
```

```python
import functools

import jax
import jax.numpy as jnp
from jax import lax
from jax.experimental import pallas as pl
from jax.experimental.pallas import tpu as pltpu
from jax.sharding import PartitionSpec as P

COLS = 64
TILE = 8
MESH = pl.DeviceIdType.MESH
FAR = -1e30
K, V, Q, G = range(4)


def dot(left, right):
    return jnp.dot(left, right, preferred_element_type=jnp.float32)


def dot_nt(left, right):
    return lax.dot_general(left, right, (((1,), (1,)), ((), ())), preferred_element_type=jnp.float32)


def kernel(
    heads,
    groups,
    frames,
    window_hbm,
    k_ref,
    v_ref,
    q_ref,
    g_ref,
    o_ref,
    dq_ref,
    dk_ref,
    dv_ref,
    g_own,
    o_own,
    delta_out,
    delta_in,
    kv,
    qg,
    k_turned,
    bias,
    scores,
    dq_turned,
    acc,
    parts,
    back,
    zout,
    window_ref,
    own_sems,
    delta_sems,
    zin_send,
    zin_recv,
    halo_send,
    halo_recv,
    back_send,
    back_recv,
    zout_send,
    zout_recv,
    met,
):
    per_group = heads // groups
    width = kv.shape[-1]
    scale = width**-0.5
    me = lax.axis_index("head")
    here = lax.axis_index("frame")
    spots = frames // 2
    low, spot = here // spots, lax.rem(here, spots)
    high, core = me // 2, lax.rem(me, 2)
    frame = core * spots + spot
    group = high * 2 + low
    same = core == low
    pairs = kv.shape[5]
    size = groups * kv.shape[4] * kv.shape[6]

    def worker(g):
        return (g // 2 * 2 + low, lax.rem(g, 2) * spots + spot)

    def neighbour(f):
        return (high * 2 + f // spots, low * spots + lax.rem(f, spots))

    up = neighbour(lax.rem(frame + 1, frames))
    down = neighbour(lax.rem(frame + frames - 1, frames))

    barrier = pltpu.get_barrier_semaphore()

    @pl.when(jnp.logical_not(same))
    def _():
        pl.semaphore_signal(barrier, 1, device_id=worker(group), device_id_type=MESH)

    for step in range(1, groups):
        pl.semaphore_signal(
            barrier, 1, device_id=worker(lax.rem(group + step, groups)), device_id_type=MESH
        )
    for i in range(groups // 2):
        pl.semaphore_signal(barrier, 1, device_id=(2 * i + 1 - low, frame), device_id_type=MESH)
    at_end = spot == spots - 1
    at_start = spot == 0

    def signal(condition, sem, other):
        @pl.when(condition)
        def _():
            pl.semaphore_signal(sem, 1, device_id=other, device_id_type=MESH)

    signal(jnp.logical_not(at_end), barrier, up)
    signal(at_start, barrier, down)
    own = [
        pltpu.make_async_copy(g_ref, g_own, own_sems.at[0]),
        pltpu.make_async_copy(o_ref, o_own, own_sems.at[1]),
        pltpu.make_async_copy(window_hbm, window_ref, own_sems.at[2]),
    ]
    for copy in own:
        copy.start()

    count = groups - 1 + groups // 2 + jnp.where(same, 0, 1)
    pl.semaphore_wait(barrier, count + jnp.where(at_start, 0, 1) + jnp.where(at_end, 1, 0))
    signal(jnp.logical_not(at_start), met.at[0], down)
    signal(at_end, met.at[1], up)

    def landing(array, head):
        return kv.at[0, array, head] if array < 2 else qg.at[array - 2, head]

    def move(stays, src, dst, send, recv, to):
        def remote():
            pltpu.make_async_remote_copy(
                src_ref=src, dst_ref=dst, send_sem=send, recv_sem=recv, device_id=to, device_id_type=MESH
            ).start()

        if stays is None:
            remote()
        else:
            pl.when(jnp.logical_not(stays))(remote)

            @pl.when(stays)
            def _():
                pltpu.make_async_copy(src, dst, recv).start()

    def wait_sent(ref, sem):
        rest = ref.at[1:groups]
        pltpu.make_async_copy(rest, rest, sem).wait()

        @pl.when(jnp.logical_not(same))
        def _():
            pltpu.make_async_copy(ref.at[0], ref.at[0], sem).wait()

    def send_in(array, head):
        ref = (k_ref, v_ref, q_ref, g_ref)[array]
        for step in range(groups):
            to = lax.rem(group + step, groups)
            column = pl.multiple_of((to * per_group + head) * width, width)
            move(
                same if step == 0 else None,
                ref.at[:, :, :, pl.ds(column, width)],
                landing(array, head).at[me],
                zin_send.at[array, head],
                zin_recv.at[array, head],
                worker(to),
            )

    def arrived(array, head):
        ref = landing(array, head)
        pltpu.make_async_copy(ref, ref, zin_recv.at[array, head]).wait()

    for array in (K, V, Q):
        send_in(array, 0)

    for copy in own:
        copy.wait()
    lane = lax.broadcasted_iota(jnp.int32, (1, 128), 1)
    place = lax.rem(me, 4) * 32
    for h in range(heads):
        cols = slice(h * width, (h + 1) * width)
        product = g_own[:, :, :, cols].astype(jnp.float32) * o_own[:, :, :, cols].astype(jnp.float32)
        turned = product.reshape(128, width).T
        row = jnp.sum(turned, axis=0, keepdims=True)
        for m in range(pairs):
            first = pltpu.roll(row, lax.rem(place + 128 - m * 16, 128), 1)
            second = pltpu.roll(row, lax.rem(place + 16 + 64 - m * 16, 128), 1)
            mine = lane - place
            placed = jnp.where(
                (mine >= 0) & (mine < 16),
                first,
                jnp.where((mine >= 16) & (mine < 32), second, 0.0),
            )
            at = (h % per_group) * pairs + m
            delta_out[h // per_group, at : at + 1, :] = placed
    for step in range(groups):
        to = lax.rem(group + step, groups)
        move(same if step == 0 else None, delta_out.at[to], delta_in.at[me], delta_sems.at[0], delta_sems.at[1], worker(to))

    k_at = lax.broadcasted_iota(jnp.int32, (size, size), 0)
    q_at = lax.broadcasted_iota(jnp.int32, (size, size), 1)
    row_gap = jnp.abs(k_at // (size // 2) - q_at // (size // 2))
    for head in range(per_group):
        reach_f = window_ref[0, group * per_group + head]
        reach_h = window_ref[1, group * per_group + head]
        reach_w = window_ref[2, group * per_group + head]
        below = jnp.where((reach_f >= 1) & (frame >= 1), 0.0, FAR)
        above = jnp.where((reach_f >= 1) & (frame < frames - 1), 0.0, FAR)
        for gap in (-1, 0, 1):
            col_gap = jnp.abs(2 * gap + (k_at % 16) // 8 - (q_at % 16) // 8)
            near = jnp.where((row_gap <= reach_h) & (col_gap <= reach_w), 0.0, FAR)
            bias[head, 0, gap + 1] = near
            bias[head, 1, gap + 1] = near + below
            bias[head, 2, gap + 1] = near + above

    def halo(array, head, side):
        return pltpu.make_async_remote_copy(
            src_ref=kv.at[0, array, head],
            dst_ref=kv.at[1 + side, array, head],
            send_sem=halo_send.at[side, array, head],
            recv_sem=halo_recv.at[side, array, head],
            device_id=(up, down)[side],
            device_id_type=MESH,
        )

    def send_halo(array, head):
        arrived(array, head)
        for side in range(2):
            halo(array, head, side).start()

    def part_back(head, n, side):
        return pltpu.make_async_remote_copy(
            src_ref=parts.at[side, head, n],
            dst_ref=back.at[side, head, n],
            send_sem=back_send.at[side, head, n],
            recv_sem=back_recv.at[side, head, n],
            device_id=(down, up)[side],
            device_id_type=MESH,
        )

    outs = (dq_ref, dk_ref, dv_ref)

    def send_piece(array, head, first, count, to, stays):
        column = pl.multiple_of((group * per_group + head) * width, width)
        move(
            stays,
            zout.at[array, head, to, :, first : first + count],
            outs[array].at[:, first : first + count, :, pl.ds(column, width)],
            zout_send.at[array, head],
            zout_recv.at[array],
            (to, frame),
        )

    def send_out(array, head, first, count):
        for step in range(groups):
            stays = same if step == 0 else None
            send_piece(array, head, first, count, lax.rem(me + step, groups), stays)

    def send_last(head, first, count):
        targets = [0, 1] + [2 + lax.rem(me + step, groups - 2) for step in range(groups - 2)]
        for to in targets:
            for array in (1, 2):
                send_piece(array, head, first, count, to, same & (me == to))

    def block(ref, n):
        return ref[:, :, n].reshape(size, width)

    def turn(head, o):
        for n in range(pairs):
            k_turned[o, n] = block(kv.at[o, K, head], n).T

    def compute(head, leaving, before, after):
        for m in range(pairs):
            near = [n for n in (m - 1, m, m + 1) if 0 <= n < pairs]
            queries = block(qg.at[0, head], m)
            grads = block(qg.at[1, head], m)
            at = head * pairs + m
            halves = [
                sum(delta_in[s, at : at + 1, :] for s in range(half * 4, half * 4 + 4)) for half in range(2)
            ]
            delta = jnp.concatenate(halves, axis=1)

            def score(o, top):
                for n in near:
                    raw = dot_nt(block(kv.at[o, K, head], n), queries)
                    masked = raw * scale + bias[head, o, n - m + 1]
                    scores[o, n - m + 1] = masked
                    top = jnp.maximum(top, jnp.max(masked.reshape(size // 8, 8, size), axis=0))
                return top

            top = lax.fori_loop(0, 3, score, jnp.full((8, size), FAR, jnp.float32), unroll=True)
            top = jnp.max(top, axis=0, keepdims=True)

            def weight(o, total):
                for n in near:
                    e = jnp.exp(scores[o, n - m + 1] - top)
                    scores[o, n - m + 1] = e
                    total = total + jnp.sum(e.reshape(size // 8, 8, size), axis=0)
                return total

            total = lax.fori_loop(0, 3, weight, jnp.zeros((8, size), jnp.float32), unroll=True)
            inverse = 1.0 / jnp.sum(total, axis=0, keepdims=True)
            dq_turned[...] = jnp.zeros_like(dq_turned)

            def backward(o, nothing):
                for n in near:
                    prob = scores[o, n - m + 1] * inverse
                    prob_grad = dot_nt(block(kv.at[o, V, head], n), grads)
                    score_grad = (prob * (prob_grad - delta)).astype(jnp.bfloat16)
                    key_part = dot(score_grad, queries)
                    value_part = dot(prob.astype(jnp.bfloat16), grads)
                    if m == max(n - 1, 0):
                        acc[head, o, 0, n] = key_part
                        acc[head, o, 1, n] = value_part
                    else:
                        acc[head, o, 0, n] += key_part
                        acc[head, o, 1, n] += value_part
                    dq_turned[...] += dot(k_turned[o, n], score_grad)
                return nothing

            lax.fori_loop(0, 3, backward, 0, unroll=True)
            zout[0, head, :, :, m] = (
                (dq_turned[...] * scale).T.astype(jnp.bfloat16).reshape(zout.shape[2], zout.shape[3], 16, width)
            )
            before(m)
            for n in leaving[m]:
                for side in range(2):
                    parts[side, head, n, 0] = (acc[head, 1 + side, 0, n] * scale).astype(jnp.bfloat16)
                    parts[side, head, n, 1] = acc[head, 1 + side, 1, n].astype(jnp.bfloat16)
                    part_back(head, n, side).start()
            after(m)

    def finish(head, first, count, final=False):
        for n in range(first, first + count):
            for side in range(2):
                part_back(head, n, side).wait_recv()
            for array in range(2):
                mine = acc[head, 0, array, n]
                if array == 0:
                    mine = mine * scale
                whole = mine + back[0, head, n, array].astype(jnp.float32) + back[1, head, n, array].astype(jnp.float32)
                zout[1 + array, head, :, :, n] = whole.astype(jnp.bfloat16).reshape(
                    zout.shape[2], zout.shape[3], 16, width
                )
        if final:
            send_last(head, first, count)
        else:
            for array in range(2):
                send_out(1 + array, head, first, count)

    def halo_arrived(array, head):
        for side in range(2):
            halo(array, head, side).wait_recv()

    half = pairs // 2

    @pl.when(jnp.logical_not(at_end))
    def _():
        pl.semaphore_wait(met.at[0], 1)

    @pl.when(at_start)
    def _():
        pl.semaphore_wait(met.at[1], 1)

    send_halo(K, 0)
    send_in(G, 0)
    turn(0, 0)
    send_halo(V, 0)
    send_in(K, 1)
    arrived(Q, 0)
    send_in(V, 1)
    halo_arrived(K, 0)
    turn(0, 1)
    turn(0, 2)
    pltpu.make_async_copy(delta_in, delta_in, delta_sems.at[1]).wait()
    arrived(G, 0)
    send_in(Q, 1)
    halo_arrived(V, 0)

    def nothing(m):
        pass

    def during_first(m):
        if m == 1:
            send_halo(K, 1)
            send_in(G, 1)
        elif m == 2:
            send_halo(V, 1)

    compute(0, ((), (), (0, 1), (2, 3)), during_first, nothing)
    send_out(0, 0, 0, pairs)
    turn(1, 0)
    halo_arrived(K, 1)
    turn(1, 1)
    turn(1, 2)
    arrived(Q, 1)
    arrived(G, 1)
    halo_arrived(V, 1)

    def during_second(m):
        if m < half:
            send_out(0, 1, m, 1)
        if m == 1:
            finish(0, 0, half)
        elif m == 2:
            finish(0, half, 1)

    compute(1, ((), (0,), (1,), (2, 3)), nothing, during_second)
    finish(0, half + 1, half - 1)
    send_out(0, 1, half, half)
    finish(1, 0, half, True)
    finish(1, half, half, True)

    for array in range(3):
        pltpu.make_async_copy(outs[array], outs[array], zout_recv.at[array]).wait()
    for head in range(per_group):
        for array in range(3):
            wait_sent(zout.at[array, head], zout_send.at[array, head])
        for array in (K, V, Q, G):
            wait_sent(landing(array, head), zin_send.at[array, head])
        for side in range(2):
            for array in (K, V):
                halo(array, head, side).wait_send()
            for n in range(pairs):
                part_back(head, n, side).wait_send()
    wait_sent(delta_out, delta_sems.at[0])


def settle(*refs):
    copies = [pltpu.make_async_copy(refs[i], refs[3 + i], refs[6].at[i]) for i in range(3)]
    for copy in copies:
        copy.start()
    for copy in copies:
        copy.wait()


def on_device(query, key, value, grad_out, attn_out, window):
    heads = window.shape[0]
    groups = lax.axis_size("head")
    frames = lax.axis_size("frame")
    tokens = query.shape[1]
    width = query.shape[2] // heads
    per_group = heads // groups
    rows = tokens // COLS
    pairs = COLS // (2 * TILE)
    split = (rows, pairs, 2 * TILE, query.shape[2])
    size = groups * rows * 2 * TILE
    dma = pltpu.SemaphoreType.DMA
    half = jnp.bfloat16
    full = jnp.float32
    in_hbm = pl.BlockSpec(memory_space=pltpu.HBM)
    grid = (groups, rows, pairs, 2 * TILE, width)
    outs = pl.pallas_call(
        functools.partial(kernel, heads, groups, frames),
        out_shape=[pltpu.VMEM(split, half)] * 3,
        in_specs=[in_hbm] * 6,
        out_specs=[pl.BlockSpec(memory_space=pltpu.VMEM)] * 3,
        scratch_shapes=[
            pltpu.VMEM(split, half),
            pltpu.VMEM(split, half),
            pltpu.VMEM((groups, per_group * pairs, 128), full),
            pltpu.VMEM((groups, per_group * pairs, 128), full),
            pltpu.VMEM((3, 2, per_group) + grid, half),
            pltpu.VMEM((2, per_group) + grid, half),
            pltpu.VMEM((3, pairs, width, size), half),
            pltpu.VMEM((per_group, 3, 3, size, size), full),
            pltpu.VMEM((3, 3, size, size), full),
            pltpu.VMEM((width, size), full),
            pltpu.VMEM((per_group, 3, 2, pairs, size, width), full),
            pltpu.VMEM((2, per_group, pairs, 2, size, width), half),
            pltpu.VMEM((2, per_group, pairs, 2, size, width), half),
            pltpu.VMEM((3, per_group) + grid, half),
            pltpu.SMEM((window.shape[1], heads), jnp.int32),
            dma((3,)),
            dma((2,)),
            dma((4, per_group)),
            dma((4, per_group)),
            dma((2, 2, per_group)),
            dma((2, 2, per_group)),
            dma((2, per_group, pairs)),
            dma((2, per_group, pairs)),
            dma((3, per_group)),
            dma((3,)),
            pltpu.SemaphoreType.REGULAR((2,)),
        ],
        compiler_params=pltpu.CompilerParams(
            collective_id=0, has_side_effects=True, vmem_limit_bytes=56 * 2**20
        ),
        name="tile_attention_backward",
    )(window.T, *(x.reshape(split) for x in (key, value, query, grad_out, attn_out)))
    outs = pl.pallas_call(
        settle,
        out_shape=[jax.ShapeDtypeStruct(split, half)] * 3,
        in_specs=[pl.BlockSpec(memory_space=pltpu.VMEM)] * 3,
        out_specs=[in_hbm] * 3,
        scratch_shapes=[dma((3,))],
        compiler_params=pltpu.CompilerParams(vmem_limit_bytes=8 * 2**20),
        name="settle",
    )(*outs)
    return tuple(x.reshape(query.shape) for x in outs)


def solution(mesh):
    in_specs = (
        P("frame", "head", None),
        P("frame", "head", None),
        P("frame", "head", None),
        P("frame", "head", None),
        P("frame", "head", None),
        P(),
    )
    out_specs = (P("frame", "head", None), P("frame", "head", None), P("frame", "head", None))
    return jax.shard_map(
        on_device, mesh=mesh, in_specs=in_specs, out_specs=out_specs, check_vma=False
    )
```
